32 devices in a mesh: groups: 2 (over y), rows: 4 (over x, core), cols: 4 (over z).
Axes of the slice: x: 2, y: 2, z: 4, core: 2. Of those that a mesh axis runs over, the one named last changes fastest.
Arguments:
- iterate: float32 [8192, 8192], P(('groups', 'rows'), 'cols'), parts along dimension 0, may hold values from -1 to 1
Outputs:
- update: float32 [8192, 8192], P(('groups', 'rows'), 'cols'), parts along dimension 0
The draws below stay inside these ranges and needn't reach their ends.
There are 2 independent parts, one for each index of `groups`. The reference program is written for one: setup_inputs(seed, part) draws one part's arguments, and reference() takes and returns one part's arrays. A program takes and returns all parts, laid end to end along the dimension named above; each array names one. Nothing has to cross between parts.
All inputs are finite; a program needn't handle non-finite values.
Results may differ from the reference program's by a relative error of at most 0.0042.
Values may be sent and summed in bfloat16 or wider, within the bound.
No kernel may reach another device: no remote copies, remote signals or barrier semaphores. Data moves between devices by JAX's collectives and lax.ppermute only.
A program may use at most 128 MiB of HBM per device.

```python
import math
import jax
import jax.numpy as jnp
from jax import lax

HEIGHT = 4096
BREADTH = 8192


def draw_iterate(key, part):
    key = jax.random.fold_in(key, 11)
    spread = 0.95 / (math.sqrt(HEIGHT) + math.sqrt(BREADTH))
    values = jnp.clip(jax.random.normal(key, (HEIGHT, BREADTH), jnp.float32), -6.0, 6.0)
    return values * spread


def setup_inputs(seed: int = 0, part: int = 0) -> dict:
    key_of = jax.random.split(jax.random.key(seed), 2)
    part_keys = jax.random.split(jax.random.fold_in(key_of[1], part), 2)
    iterate = draw_iterate(jax.random.fold_in(jax.random.fold_in(key_of[1], part), 71), part)
    return dict(iterate=iterate)


coef_a = 3.4445
coef_b = -4.775
coef_c = 2.0315

def reference(iterate):
    iterate_half = iterate.astype(jnp.bfloat16)
    gram = lax.dot_general(iterate_half, iterate_half, (((1,), (1,)), ((), ())), preferred_element_type=jnp.float32)
    gram_half = gram.astype(jnp.bfloat16)
    square = jnp.dot(gram_half, gram_half, preferred_element_type=jnp.float32)
    poly = (coef_b * gram + coef_c * square).astype(jnp.bfloat16)
    applied = jnp.dot(poly, iterate_half, preferred_element_type=jnp.float32)
    factor = 0.2 * math.sqrt(max(HEIGHT, BREADTH))
    return factor * (coef_a * iterate + applied)
```

```python
import math

import jax
import jax.numpy as jnp
from jax import lax
from jax.sharding import PartitionSpec as P

HEIGHT = 4096
BREADTH = 8192

coef_a = 3.4445
coef_b = -4.775
coef_c = 2.0315

WIDTH = 256
SKEW = 1

NT = (((1,), (1,)), ((), ()))


def solution(mesh):
    rows = mesh.shape["rows"]
    cols = mesh.shape["cols"]

    def swap(value, mask):
        return lax.ppermute(value, "rows", [(i, i ^ mask) for i in range(rows)])

    def shift(value, by):
        pairs = [(i, i + by) for i in range(cols) if 0 <= i + by < cols]
        return lax.ppermute(value, "cols", pairs)

    def after(value, *others):
        return lax.optimization_barrier((value, *others))[0]

    def nt(a, b):
        return lax.dot_general(a, b, NT, preferred_element_type=jnp.float32)

    def dot(a, b):
        return jnp.dot(a, b, preferred_element_type=jnp.float32)

    def choose(index, options):
        out = None
        for k, o in enumerate(options):
            if o is None:
                continue
            out = jnp.where(index == k, o, jnp.zeros_like(o) if out is None else out)
        return out

    def on_device(iterate):
        m, n = iterate.shape
        pieces = max(1, m // WIDTH)
        w = m // pieces
        z = lax.axis_index("cols")
        zz = cols - 1 - z
        x0 = iterate.astype(jnp.bfloat16)

        parts = {}
        for i in range(pieces):
            parts[0, i] = x0[i * w : (i + 1) * w]
            parts[1, i] = swap(parts[0, i], 1)
        order = [(t, i) for t in (0, 1) for i in range(pieces)]
        crossed = []
        for t in range(2, rows, 2):
            for i in range(pieces):
                piece = parts[0, i]
                if len(crossed) >= 2:
                    piece = after(piece, crossed[-2])
                parts[t, i] = swap(piece, t)
                crossed.append(parts[t, i])
                parts[t + 1, i] = swap(parts[t, i], 1)
                order += [(t, i), (t + 1, i)]

        own = [nt(x0, parts[k]).astype(jnp.bfloat16) for k in order]
        count = len(order)

        def at(values, j):
            return values[j] if 0 <= j < len(values) else None

        got_r, got_l = [], []
        whole, rest = {}, {}
        sib, far = {}, {}

        def finish(j):
            total = own[j].astype(jnp.float32)
            for index, got in ((z, got_r), (zz, got_l)):
                came = choose(
                    index,
                    [None] + [at(got, j + SKEW * (k - 1)) for k in range(1, cols)],
                )
                total = total + came.astype(jnp.float32)
            key = order[j]
            whole[key] = total.astype(jnp.bfloat16)
            rest[key] = (total - whole[key].astype(jnp.float32)).astype(jnp.bfloat16)
            sib[key] = swap(whole[key], 1)
            v, i = key
            for t in range(2, rows, 2):
                if (t ^ v) >= 2:
                    piece = whole[key]
                    piece = after(piece, crossed[-2])
                    far[t, v, i] = swap(piece, t)
                    crossed.append(far[t, v, i])
                    far[t + 1, v, i] = swap(far[t, v, i], 1)

        for s in range(count + SKEW * (cols - 2)):
            for index, got, by in ((z, got_r, 1), (zz, got_l, -1)):
                mine = choose(index, [at(own, s - SKEW * k) for k in range(cols - 1)])
                before = at(got, s - SKEW)
                if before is not None:
                    mine = mine.astype(jnp.float32) + before.astype(jnp.float32)
                got.append(shift(mine.astype(jnp.bfloat16), by))
            if s >= SKEW * (cols - 2):
                finish(s - SKEW * (cols - 2))

        def joined(pick):
            return jnp.concatenate([pick(i) for i in range(pieces)], axis=1)

        mine = [joined(lambda i: whole[t, i]) for t in range(rows)]
        beside = [joined(lambda i: sib[t, i]) for t in range(rows)]

        def block(t, u):
            if t == 0:
                return mine[u]
            if t == 1:
                return beside[u ^ 1]
            return joined(lambda i: far[t, t ^ u, i])

        poly = []
        for u in range(rows):
            square = None
            for t in range(rows):
                term = nt(mine[t], block(u, t)) if u < 2 else dot(mine[t], block(t, u))
                square = term if square is None else square + term
            gram = joined(
                lambda i: whole[u, i].astype(jnp.float32)
                + rest[u, i].astype(jnp.float32)
            )
            poly.append((coef_b * gram + coef_c * square).astype(jnp.bfloat16))
        applied = None
        for u in range(rows):
            there = jnp.concatenate([parts[u, i] for i in range(pieces)], axis=0)
            term = dot(poly[u], there)
            applied = term if applied is None else applied + term
        factor = 0.2 * math.sqrt(max(HEIGHT, BREADTH))
        return factor * (coef_a * iterate + applied)

    return jax.shard_map(
        on_device,
        mesh=mesh,
        in_specs=(P(("groups", "rows"), "cols"),),
        out_specs=P(("groups", "rows"), "cols"),
        check_vma=False,
    )
```

```python
import functools
import math

import jax
import jax.numpy as jnp
from jax import lax
from jax.experimental import pallas as pl
from jax.experimental.pallas import tpu as pltpu
from jax.sharding import PartitionSpec as P

HEIGHT = 4096
BREADTH = 8192

coef_a = 3.4445
coef_b = -4.775
coef_c = 2.0315

PIECES = 2
WIDTH = 256
SKEW = 2
TILE = 256
STRIPE = 512

NN = (((1,), (0,)), ((), ()))
NT = (((1,), (1,)), ((), ()))


def dots_body(flips, scales, out_scale, height, *refs):
    count = len(flips)
    pairs, adds, out = refs[: 2 * count], refs[2 * count : -1], refs[-1]
    for start in range(0, out.shape[0], height):
        here = pl.ds(start, height)
        total = None
        for k in range(count):
            term = lax.dot_general(
                pairs[2 * k][here, :],
                pairs[2 * k + 1][...],
                NT if flips[k] else NN,
                preferred_element_type=jnp.float32,
            )
            total = term if total is None else total + term
        if scales[0] != 1.0:
            total = scales[0] * total
        for scale, add in zip(scales[1:], adds):
            value = add[here, :].astype(jnp.float32)
            total = total + (value if scale == 1.0 else scale * value)
        if out_scale != 1.0:
            total = out_scale * total
        out[here, :] = total.astype(out.dtype)


def dots(pairs, width, tile, dot_scale, adds, out_dtype, out_scale=1.0):
    m = pairs[0][0].shape[0]
    operands, specs, flips = [], [], []
    flops = 0
    for left, column, depth, right, where in pairs:
        operands += [left, right]
        specs.append(
            pl.BlockSpec(
                (m, depth),
                functools.partial(lambda c, j: (0, c), column),
                pipeline_mode=pl.Buffered(1),
            )
        )
        flip = callable(where)
        if flip:
            specs.append(
                pl.BlockSpec(
                    (tile, depth), functools.partial(lambda f, j: (f(j), 0), where)
                )
            )
        else:
            specs.append(
                pl.BlockSpec(
                    (depth, tile), functools.partial(lambda b, j: (b, j), where)
                )
            )
        flips.append(flip)
        flops += 2 * m * depth * width
    for _, add in adds:
        operands.append(add)
        specs.append(pl.BlockSpec((m, tile), lambda j: (0, j)))
    moved = sum(o.size * o.dtype.itemsize for o in operands)
    return pl.pallas_call(
        functools.partial(
            dots_body,
            tuple(flips),
            (dot_scale,) + tuple(s for s, _ in adds),
            out_scale,
            min(STRIPE, m),
        ),
        out_shape=jax.ShapeDtypeStruct((m, width), out_dtype),
        grid=(width // tile,),
        in_specs=specs,
        out_specs=pl.BlockSpec((m, tile), lambda j: (0, j)),
        compiler_params=pltpu.CompilerParams(vmem_limit_bytes=36 * 1024 * 1024),
        cost_estimate=pl.CostEstimate(
            flops=flops, bytes_accessed=moved, transcendentals=0
        ),
    )(*operands)


def gate_body(*refs):
    pass


def gate(values):
    anywhere = pl.BlockSpec(memory_space=pl.ANY)
    return list(
        pl.pallas_call(
            gate_body,
            out_shape=[jax.ShapeDtypeStruct(v.shape, v.dtype) for v in values],
            in_specs=[anywhere] * len(values),
            out_specs=[anywhere] * len(values),
            input_output_aliases={k: k for k in range(len(values))},
            cost_estimate=pl.CostEstimate(flops=0, bytes_accessed=0, transcendentals=0),
        )(*values)
    )


def solution(mesh):
    rows = mesh.shape["rows"]
    cols = mesh.shape["cols"]
    chips = rows // 2

    def swap(value, mask):
        return lax.ppermute(value, "rows", [(i, i ^ mask) for i in range(rows)])

    def side(value):
        pairs = [[2 * i, 2 * i + 1] for i in range(chips)]
        return lax.all_gather(
            value, "rows", axis=0, tiled=True, axis_index_groups=pairs
        )

    def trade(value, start):
        pairs = []
        for i in range(start, cols - 1, 2):
            pairs += [(i, i + 1), (i + 1, i)]
        return lax.ppermute(value, "cols", pairs)

    def choose(index, options):
        out = None
        for k, o in options:
            out = o if out is None else jnp.where(index == k, o, out)
        return out

    def wide(value):
        return value.astype(jnp.float32)

    def on_device(iterate):
        m, n = iterate.shape
        mp = m // PIECES
        w = min(WIDTH, 2 * mp)
        q = 2 * mp // w
        tile = min(TILE, mp)
        z = lax.axis_index("cols")
        even = jnp.where(z % 2 == 0, z, cols - 1 - z)
        odd = cols - 1 - even
        x0 = iterate.astype(jnp.bfloat16)
        zero = jnp.zeros((m, w), jnp.bfloat16)

        groups = [(d, p) for d in range(chips) for p in range(PIECES)]
        order = [(g, i) for g in groups for i in range(q)]
        count = len(order)
        lag = SKEW * (cols - 2)
        steps = count + lag
        ready = {
            g: order.index((g, q - 1)) + lag + SKEW for g in groups
        }

        held = {}
        passing = {s: [] for s in range(steps + 1)}
        follow = {s: [] for s in range(steps + 1)}

        def hold(key, value, s):
            held[key] = value
            if 0 <= s < steps:
                passing[s].append(key)

        def then(s, action):
            if 0 <= s < steps:
                follow[s].append(action)
            else:
                late.append(action)

        late = []
        blocks = {}

        def cross(key):
            d, p = key
            held["x", key] = swap(held.pop(("x0", key)), 2 * d)

        def settle(key):
            blocks[key] = side(held.pop(("x", key)))

        for g in groups:
            d, p = g
            piece = x0[p * mp : (p + 1) * mp]
            if d == 0:
                blocks[g] = side(piece)
                continue
            i = (d - 1) * PIECES + p
            begin, end = i * q - 1, (i + 1) * q
            hold(("x0", g), piece, begin)
            if begin < 0:
                cross(g)
            else:
                then(begin, functools.partial(cross, g))
            passing[end].append(("x", g))
            then(end, functools.partial(settle, g))

        own, got_e, got_o, chunks = [], {}, {}, {}
        strip, chip, far = {}, {}, {}

        def at(values, j):
            if isinstance(values, dict):
                return values.get(j, zero)
            return values[j] if 0 <= j < len(values) else zero

        def finish(j):
            came_e = choose(
                even,
                [
                    (k, at(got_e, j + SKEW * (cols - 2 - k)))
                    for k in range(0, cols - 1, 2)
                ],
            )
            came_o = choose(
                even,
                [(0, zero)]
                + [(k, at(got_o, j + SKEW * (k - 1))) for k in range(2, cols - 1, 2)],
            )
            chunks[order[j]] = (wide(own[j]) + wide(came_e) + wide(came_o)).astype(
                jnp.bfloat16
            )

        def launch(g, s):
            d0, p = g
            strip[g] = held.pop(("s", g))
            chip[g] = side(strip[g])
            for d in range(1, chips):
                e = d ^ d0
                if e == 0:
                    continue
                over = swap(strip[g], 2 * d)
                if s + q < steps:
                    hold(("f", d, e, p), over, s + q)
                    then(s + q, functools.partial(land, d, e, p))
                else:
                    far[d, e, p] = side(over)

        def land(d, e, p):
            far[d, e, p] = side(held.pop(("f", d, e, p)))

        def complete(g, s):
            held["s", g] = jnp.concatenate([chunks[g, i] for i in range(q)], axis=1)
            if s < steps:
                passing[s].append(("s", g))
                follow[s].append(functools.partial(launch, g, s))
            else:
                launch(g, s)

        poly, others = {}, {}

        def turned(p):
            per = mp // tile
            return lambda j: (j // per * PIECES + p) * per + j % per

        def poly_first(p):
            poly[p] = dots(
                [
                    (strip[0, r], 0, 2 * mp, chip[0, r], turned(p))
                    for r in range(PIECES)
                ],
                2 * mp,
                tile,
                coef_c,
                [(coef_b, strip[0, p])],
                jnp.float32,
            )

        def poly_next(r, p):
            poly[p] = dots(
                [
                    (strip[d, r], 0, 2 * mp, chip[d, r], turned(p))
                    for d in range(1, chips)
                ],
                2 * mp,
                tile,
                coef_c,
                [(1.0, poly[p])],
                jnp.bfloat16 if r == PIECES - 1 else jnp.float32,
            )

        def others_next(r, e, p):
            pairs = [
                (strip[d, r], c, mp, far[d, e, p], c * PIECES + r)
                for d in range(1, chips)
                for c in range(2)
            ]
            adds = [] if r == 0 else [(1.0, others[e, p])]
            if r == p:
                pairs += [
                    (strip[0, t], c, mp, chip[e, p], c * PIECES + t)
                    for t in range(PIECES)
                    for c in range(2)
                ]
                adds += [(coef_b, strip[e, p])]
            others[e, p] = dots(
                pairs,
                2 * mp,
                tile,
                coef_c,
                adds,
                jnp.bfloat16 if r == PIECES - 1 else jnp.float32,
            )

        def early(p, s):
            poly_first(p)
            if s + 1 < steps:
                held["poly", p] = poly[p]
                passing[s + 1].append(("poly", p))
                follow[s + 1].insert(0, functools.partial(regain, p))

        def regain(p):
            poly[p] = held.pop(("poly", p))

        first_at = ready[0, PIECES - 1] + 2
        for p in range(PIECES):
            then(first_at + p, functools.partial(early, p, first_at + p))

        token = jnp.zeros((8, 128), jnp.float32)
        for s in range(steps):
            if s < count:
                g, i = order[s]
                own.append(
                    lax.dot_general(
                        x0,
                        blocks[g][i * w : (i + 1) * w],
                        NT,
                        preferred_element_type=jnp.float32,
                    ).astype(jnp.bfloat16)
                )
            for g in groups:
                if ready[g] == s:
                    for i in range(q):
                        finish(order.index((g, i)))
                    complete(g, s)
            last_e, last_o = at(got_e, s - SKEW), at(got_o, s - SKEW)
            mine_e = choose(
                even, [(k, at(own, s - SKEW * k)) for k in range(0, cols - 1, 2)]
            )
            carry = jnp.where(even == 0, zero, last_o)
            sends = [(wide(mine_e) + wide(carry)).astype(jnp.bfloat16)]
            if SKEW <= s < count + SKEW * (cols - 3):
                mine_o = choose(
                    odd, [(k, at(own, s - SKEW * k)) for k in range(1, cols - 1, 2)]
                )
                sends.append((wide(mine_o) + wide(last_e)).astype(jnp.bfloat16))
            keys = passing[s]
            out = gate(sends + [held[k] for k in keys] + [token])
            token = out[-1]
            got_e[s] = trade(out[0], 0)
            if len(sends) > 1:
                got_o[s] = trade(out[1], 1)
            for k, v in zip(keys, out[len(sends) : -1]):
                held[k] = v
            for action in follow[s]:
                action()
        for action in late:
            action()

        for r in range(PIECES):
            wanted = [(d, r) for d in range(chips)] if chips == 2 else groups
            for g in wanted:
                if g not in strip:
                    for i in range(q):
                        finish(order.index((g, i)))
                    complete(g, steps)
            for e in range(1, chips):
                for p in range(PIECES):
                    if p != r:
                        others_next(r, e, p)
            for p in range(PIECES):
                poly_next(r, p)
            for e in range(1, chips):
                others_next(r, e, r)
            if r < PIECES - 1 and chips == 2:
                keys = [("p", p) for p in range(PIECES)]
                keys += [(e, p) for e in range(1, chips) for p in range(PIECES)]
                values = [poly[p] if e == "p" else others[e, p] for e, p in keys]
                out = gate(values + [got_e[steps - 1], token])
                got_e[steps - 1], token = out[-2:]
                for (e, p), v in zip(keys, out):
                    if e == "p":
                        poly[p] = v
                    else:
                        others[e, p] = v

        factor = 0.2 * math.sqrt(max(HEIGHT, BREADTH))
        return dots(
            [
                (poly[p] if e == 0 else others[e, p], 0, 2 * mp, blocks[e, p], 0)
                for e in range(chips)
                for p in range(PIECES)
            ],
            n,
            tile,
            1.0,
            [(coef_a, iterate)],
            jnp.float32,
            factor,
        )

    return jax.shard_map(
        on_device,
        mesh=mesh,
        in_specs=(P(("groups", "rows"), "cols"),),
        out_specs=P(("groups", "rows"), "cols"),
        check_vma=False,
    )
```

```python
import functools
import math

import jax
import jax.numpy as jnp
from jax import lax
from jax.experimental import pallas as pl
from jax.experimental.pallas import tpu as pltpu
from jax.sharding import PartitionSpec as P

HEIGHT = 4096
BREADTH = 8192

coef_a = 3.4445
coef_b = -4.775
coef_c = 2.0315

PIECES = 2
WIDTH = 256
SKEW = 2
TILE = 256
STRIPE = 512
VMEM = 60 * 1024 * 1024
SMALL = VMEM
PARTS = 4

NN = (((1,), (0,)), ((), ()))
NT = (((1,), (1,)), ((), ()))


def dots_body(flips, scales, out_scale, height, *refs):
    count = len(flips)
    pairs, adds, out = refs[: 2 * count], refs[2 * count : -1], refs[-1]
    for start in range(0, out.shape[0], height):
        here = pl.ds(start, height)
        total = None
        for k in range(count):
            term = lax.dot_general(
                pairs[2 * k][here, :],
                pairs[2 * k + 1][...],
                NT if flips[k] else NN,
                preferred_element_type=jnp.float32,
            )
            total = term if total is None else total + term
        if scales[0] != 1.0:
            total = scales[0] * total
        for scale, add in zip(scales[1:], adds):
            value = add[here, :].astype(jnp.float32)
            total = total + (value if scale == 1.0 else scale * value)
        if out_scale != 1.0:
            total = out_scale * total
        out[here, :] = total.astype(out.dtype)


def dots(pairs, width, tile, dot_scale, adds, out_dtype, out_scale=1.0):
    m = pairs[0][0].shape[0]
    operands, specs, flips = [], [], []
    flops = 0
    for left, column, depth, right, where in pairs:
        operands += [left, right]
        specs.append(
            pl.BlockSpec(
                (m, depth),
                functools.partial(lambda c, j: (0, c), column),
                pipeline_mode=pl.Buffered(1),
            )
        )
        flip = callable(where)
        if flip:
            specs.append(
                pl.BlockSpec(
                    (tile, depth), functools.partial(lambda f, j: (f(j), 0), where)
                )
            )
        else:
            specs.append(
                pl.BlockSpec(
                    (depth, tile), functools.partial(lambda b, j: (b, j), where)
                )
            )
        flips.append(flip)
        flops += 2 * m * depth * width
    for _, add in adds:
        operands.append(add)
        specs.append(pl.BlockSpec((m, tile), lambda j: (0, j)))
    moved = sum(o.size * o.dtype.itemsize for o in operands)
    return pl.pallas_call(
        functools.partial(
            dots_body,
            tuple(flips),
            (dot_scale,) + tuple(s for s, _ in adds),
            out_scale,
            min(STRIPE, m),
        ),
        out_shape=jax.ShapeDtypeStruct((m, width), out_dtype),
        grid=(width // tile,),
        in_specs=specs,
        out_specs=pl.BlockSpec((m, tile), lambda j: (0, j)),
        compiler_params=pltpu.CompilerParams(vmem_limit_bytes=VMEM),
        cost_estimate=pl.CostEstimate(
            flops=flops, bytes_accessed=0, transcendentals=0
        ),
    )(*operands)


def gram_body(where, left, right, out):
    out[0] = lax.dot_general(
        left[...], right[...], NT, preferred_element_type=jnp.float32
    ).astype(out.dtype)


def gram(left, right, where, count, width):
    m, n = left.shape
    return pl.pallas_call(
        gram_body,
        out_shape=jax.ShapeDtypeStruct((count, m, width), jnp.bfloat16),
        grid_spec=pltpu.PrefetchScalarGridSpec(
            num_scalar_prefetch=1,
            grid=(count,),
            in_specs=[
                pl.BlockSpec(
                    (m, n), lambda j, where: (0, 0), pipeline_mode=pl.Buffered(1)
                ),
                pl.BlockSpec((width, n), lambda j, where: (where[0] + j, 0)),
            ],
            out_specs=pl.BlockSpec((1, m, width), lambda j, where: (j, 0, 0)),
        ),
        compiler_params=pltpu.CompilerParams(vmem_limit_bytes=VMEM),
        cost_estimate=pl.CostEstimate(
            flops=2 * m * n * width * count,
            bytes_accessed=0,
            transcendentals=0,
        ),
    )(where, left, right)


def mix_body(top, plan, where, *refs):
    outs = refs[-len(plan) :]
    for out, choices in zip(outs, plan):
        total = None
        for flip, options in choices:
            here = top - where[0] if flip else where[0]
            value = None
            for k, slot in options:
                if slot is None:
                    new = jnp.zeros(out.shape, jnp.float32)
                else:
                    new = refs[slot][...].reshape(out.shape).astype(jnp.float32)
                value = new if value is None else jnp.where(here == k, new, value)
            total = value if total is None else total + value
        out[...] = total.astype(out.dtype)


def mix_all(top, plan, count, idle, where, *refs):
    ins, outs = refs[:count], refs[count + idle :]
    mix_body(top, plan, where, *ins, *outs[: len(plan)])


def mix(where, top, sums, held, parts):
    sources, uses, plan = [], [], []

    def slot_of(source, use):
        if source is None:
            return None
        for k, (array, chunk) in enumerate(sources):
            if array is source[0] and chunk == source[1]:
                uses[k].append(use)
                return k
        sources.append(source)
        uses.append([use])
        return len(sources) - 1

    for terms in sums:
        plan.append(
            tuple(
                (
                    flip,
                    tuple(
                        (k, slot_of(source, (flip, k) if len(options) > 1 else None))
                        for k, source in options
                    ),
                )
                for flip, options in terms
            )
        )
    array, chunk = sources[0]
    m, w = array.shape[-2:]
    high = m // parts
    specs = []
    for (array, chunk), used in zip(sources, uses):

        def at(j, where, chunk=chunk, used=used):
            row = j
            if None not in used:
                live = False
                for flip, k in used:
                    live = live | (where[0] == (top - k if flip else k))
                row = jnp.where(live, j, 0)
            return (row, 0) if chunk is None else (chunk, row, 0)

        specs.append(pl.BlockSpec((high, w) if chunk is None else (1, high, w), at))
    anywhere = pl.BlockSpec(memory_space=pl.ANY)
    idle, count = len(held), len(sources)
    return list(
        pl.pallas_call(
            functools.partial(mix_all, top, tuple(plan), count, idle),
            out_shape=[jax.ShapeDtypeStruct((m, w), jnp.bfloat16)] * len(plan)
            + [jax.ShapeDtypeStruct(v.shape, v.dtype) for v in held],
            grid_spec=pltpu.PrefetchScalarGridSpec(
                num_scalar_prefetch=1,
                grid=(parts,),
                in_specs=specs + [anywhere] * idle,
                out_specs=[pl.BlockSpec((high, w), lambda j, where: (j, 0))] * len(plan)
                + [anywhere] * idle,
            ),
            input_output_aliases={
                1 + count + k: len(plan) + k for k in range(idle)
            },
            compiler_params=pltpu.CompilerParams(vmem_limit_bytes=SMALL),
            cost_estimate=pl.CostEstimate(
                flops=10**10, bytes_accessed=0, transcendentals=0
            ),
        )(where, *[a for a, _ in sources], *held)
    )


def gate_body(*refs):
    pass


def gate(values):
    anywhere = pl.BlockSpec(memory_space=pl.ANY)
    return list(
        pl.pallas_call(
            gate_body,
            out_shape=[jax.ShapeDtypeStruct(v.shape, v.dtype) for v in values],
            in_specs=[anywhere] * len(values),
            out_specs=[anywhere] * len(values),
            input_output_aliases={k: k for k in range(len(values))},
            compiler_params=pltpu.CompilerParams(vmem_limit_bytes=VMEM),
            cost_estimate=pl.CostEstimate(flops=0, bytes_accessed=0, transcendentals=0),
        )(*values)
    )


def solution(mesh):
    rows = mesh.shape["rows"]
    cols = mesh.shape["cols"]
    chips = rows // 2

    def swap(value, mask):
        return lax.ppermute(value, "rows", [(i, i ^ mask) for i in range(rows)])

    def side(value):
        pairs = [[2 * i, 2 * i + 1] for i in range(chips)]
        return lax.all_gather(
            value, "rows", axis=0, tiled=True, axis_index_groups=pairs
        )

    def trade(value, start):
        pairs = []
        for i in range(start, cols - 1, 2):
            pairs += [(i, i + 1), (i + 1, i)]
        return lax.ppermute(value, "cols", pairs)

    def on_device(iterate):
        m, n = iterate.shape
        mp = m // PIECES
        w = min(WIDTH, mp)
        q = 2 * mp // w
        tile = min(TILE, mp)
        z = lax.axis_index("cols")
        core = lax.axis_index("rows") % 2
        even = jnp.where(z % 2 == 0, z, cols - 1 - z)
        where = jnp.reshape(even, (1,)).astype(jnp.int32)
        x0 = iterate.astype(jnp.bfloat16)

        groups = [(d, p) for d in range(chips) for p in range(PIECES)]
        order = [(g, i) for g in groups for i in range(q)]
        count = len(order)
        lag = SKEW * (cols - 2)
        steps = count + lag
        ready = {
            g: order.index((g, q - 1)) + lag + SKEW for g in groups
        }

        held = {}
        passing = {s: [] for s in range(steps + 1)}
        follow = {s: [] for s in range(steps + 1)}

        def hold(key, value, s):
            held[key] = value
            if 0 <= s < steps:
                passing[s].append(key)

        def then(s, action):
            if 0 <= s < steps:
                follow[s].append(action)
            else:
                late.append(action)

        late = []
        blocks = {}

        def cross(key):
            d, p = key
            held["x", key] = swap(held.pop(("x0", key)), 2 * d)

        def settle(key):
            blocks[key] = side(held.pop(("x", key)))

        for g in groups:
            d, p = g
            piece = x0[p * mp : (p + 1) * mp]
            if d == 0:
                blocks[g] = side(piece)
                continue
            i = (d - 1) * PIECES + p
            begin, end = i * q - 1, (i + 1) * q
            hold(("x0", g), piece, begin)
            if begin < 0:
                cross(g)
            else:
                then(begin, functools.partial(cross, g))
            passing[end].append(("x", g))
            then(end, functools.partial(settle, g))

        own, sent, got_e, got_o, chunks = [], {}, {}, {}, {}
        strip, chip, far = {}, {}, {}

        def at(values, j):
            if isinstance(values, dict):
                return (values[j], None) if j in values else None
            return values[j] if 0 <= j < len(values) else None

        def at_row(chunk):
            return jnp.full((1,), chunk, jnp.int32)

        def final(j):
            return [
                (
                    False,
                    [(k, at(sent, j + SKEW * k)) for k in range(0, cols - 1, 2)],
                ),
                (
                    False,
                    [
                        (k, at(got_e, j + SKEW * (cols - 2 - k)))
                        for k in range(0, cols - 1, 2)
                    ],
                ),
            ]

        def launch(g, s):
            d0, p = g
            strip[g] = held.pop(("s", g))
            chip[g] = side(strip[g])
            for d in range(1, chips):
                e = d ^ d0
                if e == 0:
                    continue
                over = swap(strip[g], 2 * d)
                if s + q < steps:
                    hold(("f", d, e, p), over, s + q)
                    then(s + q, functools.partial(land, d, e, p))
                else:
                    far[d, e, p] = side(over)

        def land(d, e, p):
            far[d, e, p] = side(held.pop(("f", d, e, p)))

        def complete(g, s):
            parts = [chunks[g, i] for i in range(q)]
            if g[0] == 0:
                near, beside = parts[: q // 2], parts[q // 2 :]
                parts = [jnp.where(core == 0, a, b) for a, b in zip(near, beside)]
                parts += [jnp.where(core == 0, b, a) for a, b in zip(near, beside)]
            held["s", g] = jnp.concatenate(parts, axis=1)
            launch(g, s)

        poly, others = {}, {}

        def turned(p):
            per = mp // tile
            return lambda j: (j // per * PIECES + p) * per + j % per

        def poly_first(p):
            poly[p] = dots(
                [
                    (strip[0, r], 0, 2 * mp, chip[0, r], turned(p))
                    for r in range(PIECES)
                ],
                2 * mp,
                tile,
                coef_c,
                [(coef_b, strip[0, p])],
                jnp.float32,
            )

        def poly_next(r, p):
            poly[p] = dots(
                [
                    (strip[d, r], 0, 2 * mp, chip[d, r], turned(p))
                    for d in range(1, chips)
                ],
                2 * mp,
                tile,
                coef_c,
                [(1.0, poly[p])],
                jnp.bfloat16 if r == PIECES - 1 else jnp.float32,
            )

        def others_next(r, e, p):
            pairs = [
                (strip[d, r], c, mp, far[d, e, p], c * PIECES + r)
                for d in range(1, chips)
                for c in range(2)
            ]
            adds = [] if r == 0 else [(1.0, others[e, p])]
            if r == p:
                pairs += [
                    (strip[0, t], c, mp, chip[e, p], c * PIECES + t)
                    for t in range(PIECES)
                    for c in range(2)
                ]
                adds += [(coef_b, strip[e, p])]
            others[e, p] = dots(
                pairs,
                2 * mp,
                tile,
                coef_c,
                adds,
                jnp.bfloat16 if r == PIECES - 1 else jnp.float32,
            )

        def early(p, s):
            poly_first(p)
            if s + 1 < steps:
                held["poly", p] = poly[p]
                passing[s + 1].append(("poly", p))
                follow[s + 1].insert(0, functools.partial(regain, p))

        def regain(p):
            poly[p] = held.pop(("poly", p))

        first_at = ready[0, PIECES - 1] + 2
        for p in range(PIECES):
            then(first_at + p, functools.partial(early, p, first_at + p))

        token = jnp.zeros((8, 128), jnp.float32)
        for s in range(steps):
            if s < count:
                g, i = order[s]
                d, p = g
                near = q // 2
                made = None
                if d == 0 and i == 0:
                    made = gram(x0, x0, at_row(p * near), near, w)
                elif d == 0 and i == near:
                    made = gram(x0, blocks[g], at_row((1 - core) * near), near, w)
                elif d > 0 and i == 0:
                    made = gram(x0, blocks[g], at_row(0), q, w)
                if made is not None:
                    own += [(made, c) for c in range(made.shape[0])]
            evens, odds = range(0, cols - 1, 2), range(1, cols - 1, 2)
            last_e, last_o = at(got_e, s - SKEW), at(got_o, s - SKEW)
            sums = [
                [
                    (False, [(k, at(own, s - SKEW * k)) for k in evens]),
                    (False, [(k, last_o if k else None) for k in evens]),
                ]
            ]
            if SKEW <= s < count + SKEW * (cols - 3):
                sums.append(
                    [
                        (True, [(k, at(own, s - SKEW * k)) for k in odds]),
                        (True, [(cols, last_e)]),
                    ]
                )
            sends = len(sums)
            j = s - lag - SKEW
            if j >= 0:
                sums.append(final(j))
            keys = passing[s]
            out = mix(where, cols - 1, sums, [held[k] for k in keys] + [token], PARTS)
            if j >= 0:
                chunks[order[j]] = out[sends]
            token = out[-1]
            sent[s] = out[0]
            got_e[s] = trade(out[0], 0)
            if sends > 1:
                got_o[s] = trade(out[1], 1)
            for k, v in zip(keys, out[len(sums) : -1]):
                held[k] = v
            for g in groups:
                if ready[g] == s:
                    complete(g, s)
            for action in follow[s]:
                action()
        for action in late:
            action()

        for r in range(PIECES):
            wanted = [(d, r) for d in range(chips)] if chips == 2 else groups
            for g in wanted:
                if g not in strip:
                    for i in range(q):
                        if (g, i) not in chunks:
                            j = order.index((g, i))
                            chunks[g, i] = mix(where, cols - 1, [final(j)], [], PARTS)[0]
                    complete(g, steps)
            for e in range(1, chips):
                for p in range(PIECES):
                    if p != r:
                        others_next(r, e, p)
            for p in range(PIECES):
                poly_next(r, p)
            for e in range(1, chips):
                others_next(r, e, r)
            if r < PIECES - 1 and chips == 2:
                keys = [("p", p) for p in range(PIECES)]
                keys += [(e, p) for e in range(1, chips) for p in range(PIECES)]
                values = [poly[p] if e == "p" else others[e, p] for e, p in keys]
                out = gate(values + [got_e[steps - 1], token])
                got_e[steps - 1], token = out[-2:]
                for (e, p), v in zip(keys, out):
                    if e == "p":
                        poly[p] = v
                    else:
                        others[e, p] = v

        factor = 0.2 * math.sqrt(max(HEIGHT, BREADTH))
        return dots(
            [
                (poly[p] if e == 0 else others[e, p], 0, 2 * mp, blocks[e, p], 0)
                for e in range(chips)
                for p in range(PIECES)
            ],
            n,
            tile,
            1.0,
            [(coef_a, iterate)],
            jnp.float32,
            factor,
        )

    return jax.shard_map(
        on_device,
        mesh=mesh,
        in_specs=(P(("groups", "rows"), "cols"),),
        out_specs=P(("groups", "rows"), "cols"),
        check_vma=False,
    )
```

```python
import functools
import math

import jax
import jax.numpy as jnp
from jax import lax
from jax.experimental import pallas as pl
from jax.experimental.pallas import tpu as pltpu
from jax.sharding import PartitionSpec as P

HEIGHT = 4096
BREADTH = 8192

coef_a = 3.4445
coef_b = -4.775
coef_c = 2.0315

PIECES = 2
WIDTH = 256
SKEW = 2
TILE = 256
HIGH = 256
VMEM = 60 * 1024 * 1024
SMALL = VMEM
PARTS = 2

NN = (((1,), (0,)), ((), ()))
NT = (((1,), (1,)), ((), ()))


def dots_body(flips, scales, out_scale, height, *refs):
    count = len(flips)
    pairs, adds, out = refs[: 2 * count], refs[2 * count : -1], refs[-1]
    for start in range(0, out.shape[0], height):
        here = pl.ds(start, height)
        total = None
        for k in range(count):
            term = lax.dot_general(
                pairs[2 * k][here, :],
                pairs[2 * k + 1][...],
                NT if flips[k] else NN,
                preferred_element_type=jnp.float32,
            )
            total = term if total is None else total + term
        if scales[0] != 1.0:
            total = scales[0] * total
        for scale, add in zip(scales[1:], adds):
            value = add[here, :].astype(jnp.float32)
            total = total + (value if scale == 1.0 else scale * value)
        if out_scale != 1.0:
            total = out_scale * total
        out[here, :] = total.astype(out.dtype)


def dots(pairs, width, tile, high, dot_scale, adds, out_dtype, out_scale=1.0, stripe=512):
    m = pairs[0][0].shape[0]
    high, once = min(high, m), {}
    if high == m:
        once["pipeline_mode"] = pl.Buffered(1)
    operands, specs, flips = [], [], []
    flops = 0
    for left, column, depth, right, where in pairs:
        operands += [left, right]
        specs.append(
            pl.BlockSpec(
                (high, depth), functools.partial(lambda c, j, i: (i, c), column), **once
            )
        )
        flip = callable(where)
        if flip:
            specs.append(
                pl.BlockSpec(
                    (tile, depth), functools.partial(lambda f, j, i: (f(j), 0), where)
                )
            )
        else:
            specs.append(
                pl.BlockSpec(
                    (depth, tile), functools.partial(lambda b, j, i: (b, j), where)
                )
            )
        flips.append(flip)
        flops += 2 * m * depth * width
    for _, add in adds:
        operands.append(add)
        specs.append(pl.BlockSpec((high, tile), lambda j, i: (i, j)))
    return pl.pallas_call(
        functools.partial(
            dots_body,
            tuple(flips),
            (dot_scale,) + tuple(s for s, _ in adds),
            out_scale,
            min(stripe, high),
        ),
        out_shape=jax.ShapeDtypeStruct((m, width), out_dtype),
        grid=(width // tile, m // high),
        in_specs=specs,
        out_specs=pl.BlockSpec((high, tile), lambda j, i: (i, j)),
        compiler_params=pltpu.CompilerParams(vmem_limit_bytes=VMEM),
        cost_estimate=pl.CostEstimate(
            flops=flops, bytes_accessed=0, transcendentals=0
        ),
    )(*operands)


def gram_body(where, *refs):
    *lefts, right, out = refs
    high = lefts[0].shape[0]
    for k, left in enumerate(lefts):
        out[0, k * high : (k + 1) * high, :] = lax.dot_general(
            left[...], right[...], NT, preferred_element_type=jnp.float32
        ).astype(out.dtype)


def gram(lefts, right, where, count, width):
    high, n = lefts[0].shape
    m = high * len(lefts)
    return pl.pallas_call(
        gram_body,
        out_shape=jax.ShapeDtypeStruct((count, m, width), jnp.bfloat16),
        grid_spec=pltpu.PrefetchScalarGridSpec(
            num_scalar_prefetch=1,
            grid=(count,),
            in_specs=[
                pl.BlockSpec(
                    (high, n), lambda j, where: (0, 0), pipeline_mode=pl.Buffered(1)
                )
            ]
            * len(lefts)
            + [pl.BlockSpec((width, n), lambda j, where: (where[0] + j, 0))],
            out_specs=pl.BlockSpec((1, m, width), lambda j, where: (j, 0, 0)),
        ),
        compiler_params=pltpu.CompilerParams(vmem_limit_bytes=VMEM),
        cost_estimate=pl.CostEstimate(
            flops=2 * m * n * width * count, bytes_accessed=0, transcendentals=0
        ),
    )(where, *lefts, right)


def mix_body(plan, count, idle, where, *refs):
    ins, outs = refs[:count], refs[count + idle :]
    for k, sums in plan:

        @pl.when(where[0] == k)
        def _():
            for out, slots in zip(outs, sums):
                total = None
                for slot in slots:
                    value = ins[slot][...].reshape(out.shape)
                    total = value if total is None else total + value
                if total is not None:
                    out[...] = total


def mix(where, sums, held, parts, strip=None):
    sources, uses = [], []
    kinds = sorted(sums[0])
    plan = []
    for k in kinds:
        row = []
        for terms in sums:
            slots = []
            for source in terms[k]:
                if source is None:
                    continue
                for slot, (array, chunk) in enumerate(sources):
                    if array is source[0] and chunk == source[1]:
                        break
                else:
                    slot = len(sources)
                    sources.append(source)
                    uses.append(set())
                uses[slot].add(k)
                slots.append(slot)
            row.append(tuple(slots))
        plan.append((k, tuple(row)))
    m, w = sources[0][0].shape[-2:]
    high = m // parts
    specs = []
    for (array, chunk), used in zip(sources, uses):

        def at(j, where, chunk=chunk, used=tuple(sorted(used))):
            row = j
            if len(used) < len(kinds):
                live = where[0] == used[0]
                for k in used[1:]:
                    live = live | (where[0] == k)
                row = jnp.where(live, j, 0)
            return (row, 0) if chunk is None else (chunk, row, 0)

        specs.append(pl.BlockSpec((high, w) if chunk is None else (1, high, w), at))
    anywhere = pl.BlockSpec(memory_space=pl.ANY)
    shapes = [jax.ShapeDtypeStruct((m, w), jnp.bfloat16)] * len(sums)
    outs = [pl.BlockSpec((high, w), lambda j, where: (j, 0))] * len(sums)
    passed = list(held)
    alias = [len(sums) + k for k in range(len(held))]
    if strip is not None:
        before, width, column = strip
        shapes[-1] = jax.ShapeDtypeStruct((m, width), jnp.bfloat16)
        outs[-1] = pl.BlockSpec((high, w), lambda j, where: (j, column(where)))
        if before is not None:
            passed.append(before)
            alias.append(len(sums) - 1)
    idle, count = len(passed), len(sources)
    return list(
        pl.pallas_call(
            functools.partial(mix_body, tuple(plan), count, idle),
            out_shape=shapes
            + [jax.ShapeDtypeStruct(v.shape, v.dtype) for v in held],
            grid_spec=pltpu.PrefetchScalarGridSpec(
                num_scalar_prefetch=1,
                grid=(parts,),
                in_specs=specs + [anywhere] * idle,
                out_specs=outs + [anywhere] * len(held),
            ),
            input_output_aliases={1 + count + k: a for k, a in enumerate(alias)},
            compiler_params=pltpu.CompilerParams(vmem_limit_bytes=SMALL),
            cost_estimate=pl.CostEstimate(
                flops=10**10, bytes_accessed=0, transcendentals=0
            ),
        )(where, *[a for a, _ in sources], *passed)
    )


def gate_body(*refs):
    pass


def gate(values, others=()):
    anywhere = pl.BlockSpec(memory_space=pl.ANY)
    return list(
        pl.pallas_call(
            gate_body,
            out_shape=[jax.ShapeDtypeStruct(v.shape, v.dtype) for v in values],
            in_specs=[anywhere] * (len(values) + len(others)),
            out_specs=[anywhere] * len(values),
            input_output_aliases={k: k for k in range(len(values))},
            compiler_params=pltpu.CompilerParams(vmem_limit_bytes=VMEM),
            cost_estimate=pl.CostEstimate(flops=0, bytes_accessed=0, transcendentals=0),
        )(*values, *others)
    )


def solution(mesh):
    rows = mesh.shape["rows"]
    cols = mesh.shape["cols"]
    chips = rows // 2

    def swap(value, mask):
        return lax.ppermute(value, "rows", [(i, i ^ mask) for i in range(rows)])

    def side(value):
        pairs = [[2 * i, 2 * i + 1] for i in range(chips)]
        return lax.all_gather(
            value, "rows", axis=0, tiled=True, axis_index_groups=pairs
        )

    def trade(value, start):
        pairs = []
        for i in range(start, cols - 1, 2):
            pairs += [(i, i + 1), (i + 1, i)]
        return lax.ppermute(value, "cols", pairs)

    def on_device(iterate):
        m, n = iterate.shape
        mp = m // PIECES
        w = min(WIDTH, mp)
        q = 2 * mp // w
        z = lax.axis_index("cols")
        core = lax.axis_index("rows") % 2
        even = jnp.where(z % 2 == 0, z, cols - 1 - z)
        where = jnp.stack([even, core]).astype(jnp.int32)
        evens = range(0, cols - 1, 2)
        x0 = [
            iterate[p * mp : (p + 1) * mp].astype(jnp.bfloat16) for p in range(PIECES)
        ]

        groups = [(d, p) for d in range(chips) for p in range(PIECES)]
        order = [(g, i) for g in groups for i in range(q)]
        count = len(order)
        lag = SKEW * (cols - 2)
        steps = count + lag
        ready = {
            g: order.index((g, q - 1)) + lag + SKEW for g in groups
        }

        held = {}
        passing = {s: [] for s in range(steps + 1)}
        follow = {s: [] for s in range(steps + 1)}

        def hold(key, value, s):
            held[key] = value
            if 0 <= s < steps:
                passing[s].append(key)

        def then(s, action):
            if 0 <= s < steps:
                follow[s].append(action)
            else:
                late.append(action)

        late = []
        blocks = {}

        crossed = []

        def behind(value):
            return gate([value], crossed[-1:])[0] if crossed else value

        def cross(key):
            d, p = key
            need = order.index((key, 0))
            crossed.append(swap(behind(held.pop(("x0", key))), 2 * d))
            hold(("b", key), side(crossed[-1]), need - 2)
            then(need - 2, functools.partial(settle, key))

        def settle(key):
            blocks[key] = held.pop(("b", key))

        for g in groups:
            d, p = g
            piece = x0[p]
            if d == 0:
                blocks[g] = side(piece)
                continue
            i = (d - 1) * PIECES + p
            begin = i * q - 1
            hold(("x0", g), piece, begin)
            if begin < 0:
                cross(g)
            else:
                then(begin, functools.partial(cross, g))

        own, sent, got_e, got_o = [], {}, {}, {}
        strip, chip, far = {}, {}, {}

        def at(values, j):
            if isinstance(values, dict):
                return (values[j], None) if j in values else None
            return values[j] if 0 <= j < len(values) else None

        def at_row(chunk):
            return jnp.full((1,), chunk, jnp.int32)

        def final(j):
            return {
                k: [at(sent, j + SKEW * k), at(got_e, j + SKEW * (cols - 2 - k))]
                for k in evens
            }

        def launch(g, s):
            d0, p = g
            strip[g] = held.pop(("s", g))
            if d0 == 0 and chips == 2:
                strip[g] = behind(strip[g])
            chip[g] = side(strip[g])
            for d in range(1, chips):
                e = d ^ d0
                if e == 0:
                    continue
                crossed.append(swap(strip[g], 2 * d))
                value = side(crossed[-1])
                if s + q + 3 < steps:
                    hold(("f", d, e, p), value, s + q + 3)
                    then(s + q + 3, functools.partial(land, d, e, p))
                else:
                    far[d, e, p] = value

        def land(d, e, p):
            far[d, e, p] = held.pop(("f", d, e, p))

        def target(j):
            (d, p), i = order[j]
            near = q // 2
            if d:
                column = lambda where: i
            elif i < near:
                column = lambda where: where[1] * near + i
            else:
                column = lambda where: (1 - where[1]) * near + i - near
            return held.get(("s", (d, p))), 2 * mp, column

        poly, others = {}, {}

        def turned(p):
            return lambda j: j * PIECES + p

        def poly_first(p):
            poly[p] = dots(
                [
                    (strip[0, r], 0, 2 * mp, chip[0, r], turned(p))
                    for r in range(PIECES)
                ],
                2 * mp,
                mp,
                HIGH,
                coef_c,
                [(coef_b, strip[0, p])],
                jnp.float32,
            )

        def poly_next(r, p):
            poly[p] = dots(
                [
                    (strip[d, r], 0, 2 * mp, chip[d, r], turned(p))
                    for d in range(1, chips)
                ],
                2 * mp,
                mp,
                HIGH,
                coef_c,
                [(1.0, poly[p])],
                jnp.bfloat16 if r == PIECES - 1 else jnp.float32,
            )

        def others_next(r, e, p):
            pairs = [
                (strip[d, r], c, mp, far[d, e, p], c * PIECES + r)
                for d in range(1, chips)
                for c in range(2)
            ]
            adds = [] if r == 0 else [(1.0, others[e, p])]
            if r == p:
                pairs += [
                    (strip[0, t], c, mp, chip[e, p], c * PIECES + t)
                    for t in range(PIECES)
                    for c in range(2)
                ]
                adds += [(coef_b, strip[e, p])]
            others[e, p] = dots(
                pairs,
                2 * mp,
                mp,
                HIGH,
                coef_c,
                adds,
                jnp.bfloat16 if r == PIECES - 1 else jnp.float32,
            )

        def early(p, s):
            poly_first(p)
            if s + 1 < steps:
                held["poly", p] = poly[p]
                passing[s + 1].append(("poly", p))
                follow[s + 1].insert(0, functools.partial(regain, p))

        def regain(p):
            poly[p] = held.pop(("poly", p))

        first_at = ready[0, PIECES - 1] + 2
        for p in range(PIECES):
            then(first_at + p, functools.partial(early, p, first_at + p))

        token = jnp.zeros((8, 128), jnp.float32)
        for s in range(steps):
            if s < count:
                g, i = order[s]
                d, p = g
                near = q // 2
                made = None
                if d == 0 and i == 0:
                    made = gram(x0, x0[p], at_row(0), near, w)
                elif d == 0 and i == near:
                    made = gram(x0, blocks[g], at_row((1 - core) * near), near, w)
                elif d > 0 and i == 0:
                    made = gram(x0, blocks[g], at_row(0), q, w)
                if made is not None:
                    own += [(made, c) for c in range(made.shape[0])]
            last_e, last_o = at(got_e, s - SKEW), at(got_o, s - SKEW)
            sums = [
                {
                    k: [at(own, s - SKEW * k)] + ([last_o] if k else [])
                    for k in evens
                }
            ]
            if SKEW <= s < count + SKEW * (cols - 3):
                sums.append(
                    {
                        k: [at(own, s - SKEW * (cols - 1 - k)), last_e] if k else []
                        for k in evens
                    }
                )
            sends = len(sums)
            j = s - lag - SKEW
            if j >= 0:
                sums.append(final(j))
            keys = passing[s]
            out = mix(
                where,
                sums,
                [held[k] for k in keys] + [token],
                PARTS,
                target(j) if j >= 0 else None,
            )
            if j >= 0:
                held["s", order[j][0]] = out[sends]
            token = out[-1]
            sent[s] = out[0]
            got_e[s] = trade(out[0], 0)
            if sends > 1:
                got_o[s] = trade(out[1], 1)
            for k, v in zip(keys, out[len(sums) : -1]):
                held[k] = v
            for g in groups:
                if ready[g] == s:
                    launch(g, s)
            for action in follow[s]:
                action()
        for action in late:
            action()

        def finish():
            for g in groups:
                if g in strip:
                    continue
                for i in range(q):
                    j = order.index((g, i))
                    if j + lag + SKEW >= steps:
                        out = mix(where, [final(j)], [], PARTS, target(j))
                        held["s", g] = out[0]
                launch(g, steps)

        far_chips = range(1, chips)
        if all((d, 0) in strip for d in far_chips):
            for p in range(PIECES):
                poly_next(0, p)
            for e in far_chips:
                others_next(0, e, 0)
            values = [poly[p] for p in range(PIECES)] + [others[e, 0] for e in far_chips]
            out = gate(values + [got_e[steps - 1], token])
            got_e[steps - 1], token = out[-2:]
            for p in range(PIECES):
                poly[p] = out[p]
            for e in far_chips:
                others[e, 0] = out[PIECES - 1 + e]
            finish()
            skip = 1
        else:
            finish()
            skip = 0
        for r in range(PIECES):
            for e in far_chips:
                for p in range(PIECES):
                    if p != r:
                        others_next(r, e, p)
            if r == 0 and skip:
                continue
            for p in range(PIECES):
                poly_next(r, p)
            for e in far_chips:
                others_next(r, e, r)

        factor = 0.2 * math.sqrt(max(HEIGHT, BREADTH))
        return dots(
            [
                (poly[p] if e == 0 else others[e, p], 0, 2 * mp, blocks[e, p], 0)
                for e in range(chips)
                for p in range(PIECES)
            ],
            n,
            TILE,
            m,
            1.0,
            [(coef_a, iterate)],
            jnp.float32,
            factor,
        )

    return jax.shard_map(
        on_device,
        mesh=mesh,
        in_specs=(P(("groups", "rows"), "cols"),),
        out_specs=P(("groups", "rows"), "cols"),
        check_vma=False,
    )
```

```python
import functools
import math

import jax
import jax.numpy as jnp
from jax import lax
from jax.experimental import pallas as pl
from jax.experimental.pallas import tpu as pltpu
from jax.sharding import PartitionSpec as P

HEIGHT = 4096
BREADTH = 8192

coef_a = 3.4445
coef_b = -4.775
coef_c = 2.0315

PIECES = 2
WIDTH = 256
SKEW = 2
TILE = 256
GAP = 4
VMEM = 60 * 1024 * 1024
SMALL = VMEM
PARTS = 2

NN = (((1,), (0,)), ((), ()))
NT = (((1,), (1,)), ((), ()))


def dots_body(flips, scales, spans, out_scale, height, *refs):
    count = len(flips)
    tile_at = pl.program_id(0)
    pairs, adds, out = refs[: 2 * count], refs[2 * count : -1], refs[-1]
    for start in range(0, out.shape[0], height):
        here = pl.ds(start, height)
        total = None
        for k in range(count):
            term = lax.dot_general(
                pairs[2 * k][here, :],
                pairs[2 * k + 1][...],
                NT if flips[k] else NN,
                preferred_element_type=jnp.float32,
            )
            total = term if total is None else total + term
        if scales[0] != 1.0:
            total = scales[0] * total
        left = list(adds)
        for scale, (number, span) in zip(scales[1:], spans):
            value = left.pop(0)[here, :]
            for k in range(1, number):
                value = jnp.where(tile_at < k * span, value, left.pop(0)[here, :])
            value = value.astype(jnp.float32)
            total = total + (value if scale == 1.0 else scale * value)
        if out_scale != 1.0:
            total = out_scale * total
        out[here, :] = total.astype(out.dtype)


def dots(pairs, width, tile, high, dot_scale, adds, out_dtype, out_scale=1.0, stripe=512):
    m = pairs[0][0].shape[0]
    high, once = min(high, m), {}
    if high == m:
        once["pipeline_mode"] = pl.Buffered(1)
    operands, specs, flips = [], [], []
    flops = 0
    for left, column, depth, right, where in pairs:
        operands += [left, right]
        specs.append(
            pl.BlockSpec(
                (high, depth), functools.partial(lambda c, j, i: (i, c), column), **once
            )
        )
        flip = callable(where)
        if flip:
            specs.append(
                pl.BlockSpec(
                    (tile, depth), functools.partial(lambda f, j, i: (f(j), 0), where)
                )
            )
        else:
            specs.append(
                pl.BlockSpec(
                    (depth, tile), functools.partial(lambda b, j, i: (b, j), where)
                )
            )
        flips.append(flip)
        flops += 2 * m * depth * width
    spans = []
    for _, joined in adds:
        span = joined[0].shape[1] // tile
        spans.append((len(joined), span))
        for k, add in enumerate(joined):
            operands.append(add)
            specs.append(
                pl.BlockSpec(
                    (high, tile),
                    functools.partial(
                        lambda f, t, j, i: (i, jnp.clip(j - f, 0, t - 1)), k * span, span
                    ),
                )
            )
    return pl.pallas_call(
        functools.partial(
            dots_body,
            tuple(flips),
            (dot_scale,) + tuple(s for s, _ in adds),
            tuple(spans),
            out_scale,
            min(stripe, high),
        ),
        out_shape=jax.ShapeDtypeStruct((m, width), out_dtype),
        grid=(width // tile, m // high),
        in_specs=specs,
        out_specs=pl.BlockSpec((high, tile), lambda j, i: (i, j)),
        compiler_params=pltpu.CompilerParams(vmem_limit_bytes=VMEM),
        cost_estimate=pl.CostEstimate(
            flops=flops, bytes_accessed=0, transcendentals=0
        ),
    )(*operands)


def gram_body(where, *refs):
    *lefts, right, out = refs
    high = lefts[0].shape[0]
    for k, left in enumerate(lefts):
        out[0, k * high : (k + 1) * high, :] = lax.dot_general(
            left[...], right[...], NT, preferred_element_type=jnp.float32
        ).astype(out.dtype)


def gram(lefts, right, where, count, width):
    high, n = lefts[0].shape
    m = high * len(lefts)
    return pl.pallas_call(
        gram_body,
        out_shape=jax.ShapeDtypeStruct((count, m, width), jnp.bfloat16),
        grid_spec=pltpu.PrefetchScalarGridSpec(
            num_scalar_prefetch=1,
            grid=(count,),
            in_specs=[
                pl.BlockSpec(
                    (high, n), lambda j, where: (0, 0), pipeline_mode=pl.Buffered(1)
                )
            ]
            * len(lefts)
            + [pl.BlockSpec((width, n), lambda j, where: (where[0] + j, 0))],
            out_specs=pl.BlockSpec((1, m, width), lambda j, where: (j, 0, 0)),
        ),
        compiler_params=pltpu.CompilerParams(vmem_limit_bytes=VMEM),
        cost_estimate=pl.CostEstimate(
            flops=2 * m * n * width * count, bytes_accessed=0, transcendentals=0
        ),
    )(where, *lefts, right)


def mix_body(plan, count, idle, where, *refs):
    ins, outs = refs[:count], refs[count + idle :]
    for k, sums in plan:

        @pl.when(where[0] == k)
        def _():
            for out, slots in zip(outs, sums):
                total = None
                for slot in slots:
                    value = ins[slot][...].reshape(out.shape)
                    total = value if total is None else total + value
                if total is not None:
                    out[...] = total


def mix(where, sums, held, parts, strip=None):
    sources, uses = [], []
    kinds = sorted(sums[0])
    plan = []
    for k in kinds:
        row = []
        for terms in sums:
            slots = []
            for source in terms[k]:
                if source is None:
                    continue
                for slot, (array, chunk) in enumerate(sources):
                    if array is source[0] and chunk == source[1]:
                        break
                else:
                    slot = len(sources)
                    sources.append(source)
                    uses.append(set())
                uses[slot].add(k)
                slots.append(slot)
            row.append(tuple(slots))
        plan.append((k, tuple(row)))
    m, w = sources[0][0].shape[-2:]
    high = m // parts
    specs = []
    for (array, chunk), used in zip(sources, uses):

        def at(j, where, chunk=chunk, used=tuple(sorted(used))):
            row = j
            if len(used) < len(kinds):
                live = where[0] == used[0]
                for k in used[1:]:
                    live = live | (where[0] == k)
                row = jnp.where(live, j, 0)
            return (row, 0) if chunk is None else (chunk, row, 0)

        specs.append(pl.BlockSpec((high, w) if chunk is None else (1, high, w), at))
    anywhere = pl.BlockSpec(memory_space=pl.ANY)
    shapes = [jax.ShapeDtypeStruct((m, w), jnp.bfloat16)] * len(sums)
    outs = [pl.BlockSpec((high, w), lambda j, where: (j, 0))] * len(sums)
    passed = list(held)
    alias = [len(sums) + k for k in range(len(held))]
    if strip is not None:
        before, width, column = strip
        shapes[-1] = jax.ShapeDtypeStruct((m, width), jnp.bfloat16)
        outs[-1] = pl.BlockSpec((high, w), lambda j, where: (j, column(where)))
        if before is not None:
            passed.append(before)
            alias.append(len(sums) - 1)
    idle, count = len(passed), len(sources)
    return list(
        pl.pallas_call(
            functools.partial(mix_body, tuple(plan), count, idle),
            out_shape=shapes
            + [jax.ShapeDtypeStruct(v.shape, v.dtype) for v in held],
            grid_spec=pltpu.PrefetchScalarGridSpec(
                num_scalar_prefetch=1,
                grid=(parts,),
                in_specs=specs + [anywhere] * idle,
                out_specs=outs + [anywhere] * len(held),
            ),
            input_output_aliases={1 + count + k: a for k, a in enumerate(alias)},
            compiler_params=pltpu.CompilerParams(vmem_limit_bytes=SMALL),
            cost_estimate=pl.CostEstimate(
                flops=4 * 10**10, bytes_accessed=0, transcendentals=0
            ),
        )(where, *[a for a, _ in sources], *passed)
    )


def solution(mesh):
    rows = mesh.shape["rows"]
    cols = mesh.shape["cols"]
    chips = rows // 2

    def swap(value, mask):
        return lax.ppermute(value, "rows", [(i, i ^ mask) for i in range(rows)])

    def side(value):
        pairs = [[2 * i, 2 * i + 1] for i in range(chips)]
        return lax.all_gather(
            value, "rows", axis=0, tiled=True, axis_index_groups=pairs
        )

    def trade(value, start):
        pairs = []
        for i in range(start, cols - 1, 2):
            pairs += [(i, i + 1), (i + 1, i)]
        return lax.ppermute(value, "cols", pairs)

    def on_device(iterate):
        m, n = iterate.shape
        mp = m // PIECES
        w = min(WIDTH, mp)
        q = 2 * mp // w
        z = lax.axis_index("cols")
        core = lax.axis_index("rows") % 2
        even = jnp.where(z % 2 == 0, z, cols - 1 - z)
        where = jnp.stack([even, core]).astype(jnp.int32)
        evens = range(0, cols - 1, 2)
        x0 = [
            iterate[p * mp : (p + 1) * mp].astype(jnp.bfloat16) for p in range(PIECES)
        ]

        groups = [(d, p) for d in range(chips) for p in range(PIECES)]
        order = [(g, i) for g in groups for i in range(q)]
        count = len(order)
        lag = SKEW * (cols - 2)
        steps = count + lag
        ready = {
            g: order.index((g, q - 1)) + lag + SKEW for g in groups
        }

        held = {}
        passing = {s: [] for s in range(steps + 1)}
        follow = {s: [] for s in range(steps + 1)}

        def hold(key, value, s):
            held[key] = value
            if 0 <= s < steps:
                passing[s].append(key)

        def then(s, action):
            if 0 <= s < steps:
                follow[s].append(action)
            else:
                late.append(action)

        late = []
        blocks = {}

        def cross(key):
            d, p = key
            end = ((d - 1) * PIECES + p + 1) * q
            hold(("x", key), swap(held.pop(("x0", key)), 2 * d), end)
            then(end, functools.partial(settle, key))

        def settle(key):
            blocks[key] = side(held.pop(("x", key)))

        for g in groups:
            d, p = g
            piece = x0[p]
            if d == 0:
                blocks[g] = side(piece)
                continue
            i = (d - 1) * PIECES + p
            begin = i * q - 1
            hold(("x0", g), piece, begin)
            if begin < 0:
                cross(g)
            else:
                then(begin, functools.partial(cross, g))

        own, sent, got_e, got_o = [], {}, {}, {}
        strip, chip, far = {}, {}, {}

        def at(values, j):
            if isinstance(values, dict):
                return (values[j], None) if j in values else None
            return values[j] if 0 <= j < len(values) else None

        def at_row(chunk):
            return jnp.full((1,), chunk, jnp.int32)

        def final(j):
            return {
                k: [at(sent, j + SKEW * k), at(got_e, j + SKEW * (cols - 2 - k))]
                for k in evens
            }

        def launch(g, s):
            d0, p = g
            strip[g] = held.pop(("s", g))
            later(("c", g), side(strip[g]), s + GAP, chip, g)
            for d in range(1, chips):
                e = d ^ d0
                if e == 0:
                    continue
                over = swap(strip[g], 2 * d)
                if s + q < steps:
                    hold(("f", d, e, p), over, s + q)
                    then(s + q, functools.partial(land, d, e, p, s + q))
                else:
                    far[d, e, p] = side(over)

        def land(d, e, p, s):
            value = side(held.pop(("f", d, e, p)))
            later(("g", d, e, p), value, s + GAP, far, (d, e, p))

        def later(key, value, s, table, place):
            if s >= steps:
                table[place] = value
                return
            hold(key, value, s)
            then(s, lambda: table.__setitem__(place, held.pop(key)))

        def target(j):
            (d, p), i = order[j]
            near = q // 2
            if d:
                column = lambda where: i
            elif i < near:
                column = lambda where: where[1] * near + i
            else:
                column = lambda where: (1 - where[1]) * near + i - near
            return held.get(("s", (d, p))), 2 * mp, column

        def turned(j):
            per = mp // TILE if mp > TILE else 1
            return ((j // per) % 2 * PIECES + j // (2 * per)) * per + j % per

        def others(e, p):
            pairs = [
                (strip[d, r], c, mp, far[d, e, p], c * PIECES + r)
                for d in range(1, chips)
                for r in range(PIECES)
                for c in range(2)
            ]
            pairs += [
                (strip[0, r], c, mp, chip[e, p], c * PIECES + r)
                for r in range(PIECES)
                for c in range(2)
            ]
            return dots(
                pairs,
                2 * mp,
                min(TILE, mp),
                m,
                coef_c,
                [(coef_b, [strip[e, p]])],
                jnp.bfloat16,
            )

        token = jnp.zeros((8, 128), jnp.float32)
        for s in range(steps):
            if s < count:
                g, i = order[s]
                d, p = g
                near = q // 2
                made = None
                if d == 0 and i == 0:
                    made = gram(x0, x0[p], at_row(0), near, w)
                elif d == 0 and i == near:
                    made = gram(x0, blocks[g], at_row((1 - core) * near), near, w)
                elif d > 0 and i == 0:
                    made = gram(x0, blocks[g], at_row(0), q, w)
                if made is not None:
                    own += [(made, c) for c in range(made.shape[0])]
            last_e, last_o = at(got_e, s - SKEW), at(got_o, s - SKEW)
            sums = [
                {
                    k: [at(own, s - SKEW * k)] + ([last_o] if k else [])
                    for k in evens
                }
            ]
            if SKEW <= s < count + SKEW * (cols - 3):
                sums.append(
                    {
                        k: [at(own, s - SKEW * (cols - 1 - k)), last_e] if k else []
                        for k in evens
                    }
                )
            sends = len(sums)
            j = s - lag - SKEW
            if j >= 0:
                sums.append(final(j))
            keys = passing[s]
            out = mix(
                where,
                sums,
                [held[k] for k in keys] + [token],
                PARTS,
                target(j) if j >= 0 else None,
            )
            if j >= 0:
                held["s", order[j][0]] = out[sends]
            token = out[-1]
            sent[s] = out[0]
            got_e[s] = trade(out[0], 0)
            if sends > 1:
                got_o[s] = trade(out[1], 1)
            for k, v in zip(keys, out[len(sums) : -1]):
                held[k] = v
            for g in groups:
                if ready[g] == s:
                    wait = 1 if g[0] == 0 and g[1] and s + 1 < steps else 0
                    if wait:
                        passing[s + 1].append(("s", g))
                        follow[s + 1].append(functools.partial(launch, g, s + 1))
                    else:
                        launch(g, s)
            for action in follow[s]:
                action()
        for action in late:
            action()

        for g in groups:
            if g in strip:
                continue
            for i in range(q):
                j = order.index((g, i))
                if j + lag + SKEW >= steps:
                    out = mix(where, [final(j)], [], PARTS, target(j))
                    held["s", g] = out[0]
            launch(g, steps)

        poly = {(e, p): others(e, p) for p in range(PIECES) for e in range(1, chips)}
        first = dots(
            [(strip[g], 0, 2 * mp, chip[g], turned) for g in groups],
            2 * m,
            min(TILE, mp),
            m,
            coef_c,
            [(coef_b, [strip[0, p] for p in range(PIECES)])],
            jnp.bfloat16,
        )
        factor = 0.2 * math.sqrt(max(HEIGHT, BREADTH))
        return dots(
            [(first, p, 2 * mp, blocks[0, p], 0) for p in range(PIECES)]
            + [(poly[g], 0, 2 * mp, blocks[g], 0) for g in groups if g[0]],
            n,
            TILE,
            m,
            1.0,
            [(coef_a, [iterate])],
            jnp.float32,
            factor,
        )

    return jax.shard_map(
        on_device,
        mesh=mesh,
        in_specs=(P(("groups", "rows"), "cols"),),
        out_specs=P(("groups", "rows"), "cols"),
        check_vma=False,
    )
```

```python
import functools
import math

import jax
import jax.numpy as jnp
from jax import lax
from jax.experimental import pallas as pl
from jax.experimental.pallas import tpu as pltpu
from jax.sharding import PartitionSpec as P

HEIGHT = 4096
BREADTH = 8192

coef_a = 3.4445
coef_b = -4.775
coef_c = 2.0315

PIECES = 2
WIDTH = 256
SKEW = 2
TILE = 256
GAP = 4
VMEM = 60 * 1024 * 1024
SMALL = VMEM
PARTS = 2

NN = (((1,), (0,)), ((), ()))
NT = (((1,), (1,)), ((), ()))


def dots_body(flips, scales, spans, out_scale, height, *refs):
    count = len(flips)
    tile_at = pl.program_id(0)
    pairs, adds, out = refs[: 2 * count], refs[2 * count : -1], refs[-1]
    for start in range(0, out.shape[0], height):
        here = pl.ds(start, height)
        total = None
        for k in range(count):
            term = lax.dot_general(
                pairs[2 * k][here, :],
                pairs[2 * k + 1][...],
                NT if flips[k] else NN,
                preferred_element_type=jnp.float32,
            )
            total = term if total is None else total + term
        if scales[0] != 1.0:
            total = scales[0] * total
        left = list(adds)
        for scale, (number, span) in zip(scales[1:], spans):
            value = left.pop(0)[here, :]
            for k in range(1, number):
                value = jnp.where(tile_at < k * span, value, left.pop(0)[here, :])
            value = value.astype(jnp.float32)
            total = total + (value if scale == 1.0 else scale * value)
        if out_scale != 1.0:
            total = out_scale * total
        out[here, :] = total.astype(out.dtype)


def dots(pairs, width, tile, high, dot_scale, adds, out_dtype, out_scale=1.0, stripe=512):
    m = pairs[0][0].shape[0]
    high, once = min(high, m), {}
    if high == m:
        once["pipeline_mode"] = pl.Buffered(1)
    operands, specs, flips = [], [], []
    flops = 0
    for left, column, depth, right, where in pairs:
        operands += [left, right]
        specs.append(
            pl.BlockSpec(
                (high, depth), functools.partial(lambda c, j, i: (i, c), column), **once
            )
        )
        flip = callable(where)
        if flip:
            specs.append(
                pl.BlockSpec(
                    (tile, depth), functools.partial(lambda f, j, i: (f(j), 0), where)
                )
            )
        else:
            specs.append(
                pl.BlockSpec(
                    (depth, tile), functools.partial(lambda b, j, i: (b, j), where)
                )
            )
        flips.append(flip)
        flops += 2 * m * depth * width
    spans = []
    for _, joined in adds:
        span = joined[0].shape[1] // tile
        spans.append((len(joined), span))
        for k, add in enumerate(joined):
            operands.append(add)
            specs.append(
                pl.BlockSpec(
                    (high, tile),
                    functools.partial(
                        lambda f, t, j, i: (i, jnp.clip(j - f, 0, t - 1)), k * span, span
                    ),
                )
            )
    return pl.pallas_call(
        functools.partial(
            dots_body,
            tuple(flips),
            (dot_scale,) + tuple(s for s, _ in adds),
            tuple(spans),
            out_scale,
            min(stripe, high),
        ),
        out_shape=jax.ShapeDtypeStruct((m, width), out_dtype),
        grid=(width // tile, m // high),
        in_specs=specs,
        out_specs=pl.BlockSpec((high, tile), lambda j, i: (i, j)),
        compiler_params=pltpu.CompilerParams(vmem_limit_bytes=VMEM),
        cost_estimate=pl.CostEstimate(
            flops=flops, bytes_accessed=0, transcendentals=0
        ),
    )(*operands)


def cast_body(source, out):
    out[...] = source[...].astype(out.dtype)


def cast(value, piece, pieces):
    m, n = value.shape
    high = m // pieces
    parts = 4
    return pl.pallas_call(
        cast_body,
        out_shape=jax.ShapeDtypeStruct((high, n), jnp.bfloat16),
        grid=(parts,),
        in_specs=[
            pl.BlockSpec((high // parts, n), lambda j: (piece * parts + j, 0))
        ],
        out_specs=pl.BlockSpec((high // parts, n), lambda j: (j, 0)),
        compiler_params=pltpu.CompilerParams(vmem_limit_bytes=VMEM),
        cost_estimate=pl.CostEstimate(flops=high * n, bytes_accessed=0, transcendentals=0),
    )(value)


def gram_body(where, *refs):
    *lefts, right, out = refs
    high = lefts[0].shape[0]
    for k, left in enumerate(lefts):
        out[0, k * high : (k + 1) * high, :] = lax.dot_general(
            left[...], right[...], NT, preferred_element_type=jnp.float32
        ).astype(out.dtype)


def gram(lefts, right, where, count, width):
    high, n = lefts[0].shape
    m = high * len(lefts)
    return pl.pallas_call(
        gram_body,
        out_shape=jax.ShapeDtypeStruct((count, m, width), jnp.bfloat16),
        grid_spec=pltpu.PrefetchScalarGridSpec(
            num_scalar_prefetch=1,
            grid=(count,),
            in_specs=[
                pl.BlockSpec(
                    (high, n), lambda j, where: (0, 0), pipeline_mode=pl.Buffered(1)
                )
            ]
            * len(lefts)
            + [pl.BlockSpec((width, n), lambda j, where: (where[0] + j, 0))],
            out_specs=pl.BlockSpec((1, m, width), lambda j, where: (j, 0, 0)),
        ),
        compiler_params=pltpu.CompilerParams(vmem_limit_bytes=VMEM),
        cost_estimate=pl.CostEstimate(
            flops=2 * m * n * width * count, bytes_accessed=0, transcendentals=0
        ),
    )(where, *lefts, right)


def mix_body(plan, count, idle, where, *refs):
    ins, outs = refs[:count], refs[count + idle :]
    for k, sums in plan:

        @pl.when(where[0] == k)
        def _():
            for out, slots in zip(outs, sums):
                total = None
                for slot in slots:
                    value = ins[slot][...].reshape(out.shape)
                    total = value if total is None else total + value
                if total is not None:
                    out[...] = total


def mix(where, sums, held, parts, strip=None):
    sources, uses = [], []
    kinds = sorted(sums[0])
    plan = []
    for k in kinds:
        row = []
        for terms in sums:
            slots = []
            for source in terms[k]:
                if source is None:
                    continue
                for slot, (array, chunk) in enumerate(sources):
                    if array is source[0] and chunk == source[1]:
                        break
                else:
                    slot = len(sources)
                    sources.append(source)
                    uses.append(set())
                uses[slot].add(k)
                slots.append(slot)
            row.append(tuple(slots))
        plan.append((k, tuple(row)))
    m, w = sources[0][0].shape[-2:]
    high = m // parts
    specs = []
    for (array, chunk), used in zip(sources, uses):

        def at(j, where, chunk=chunk, used=tuple(sorted(used))):
            row = j
            if len(used) < len(kinds):
                live = where[0] == used[0]
                for k in used[1:]:
                    live = live | (where[0] == k)
                row = jnp.where(live, j, 0)
            return (row, 0) if chunk is None else (chunk, row, 0)

        specs.append(pl.BlockSpec((high, w) if chunk is None else (1, high, w), at))
    anywhere = pl.BlockSpec(memory_space=pl.ANY)
    shapes = [jax.ShapeDtypeStruct((m, w), jnp.bfloat16)] * len(sums)
    outs = [pl.BlockSpec((high, w), lambda j, where: (j, 0))] * len(sums)
    passed = list(held)
    alias = [len(sums) + k for k in range(len(held))]
    if strip is not None:
        before, width, column = strip
        shapes[-1] = jax.ShapeDtypeStruct((m, width), jnp.bfloat16)
        outs[-1] = pl.BlockSpec((high, w), lambda j, where: (j, column(where)))
        if before is not None:
            passed.append(before)
            alias.append(len(sums) - 1)
    idle, count = len(passed), len(sources)
    return list(
        pl.pallas_call(
            functools.partial(mix_body, tuple(plan), count, idle),
            out_shape=shapes
            + [jax.ShapeDtypeStruct(v.shape, v.dtype) for v in held],
            grid_spec=pltpu.PrefetchScalarGridSpec(
                num_scalar_prefetch=1,
                grid=(parts,),
                in_specs=specs + [anywhere] * idle,
                out_specs=outs + [anywhere] * len(held),
            ),
            input_output_aliases={1 + count + k: a for k, a in enumerate(alias)},
            compiler_params=pltpu.CompilerParams(vmem_limit_bytes=SMALL),
            cost_estimate=pl.CostEstimate(
                flops=4 * 10**10, bytes_accessed=0, transcendentals=0
            ),
        )(where, *[a for a, _ in sources], *passed)
    )


def solution(mesh):
    rows = mesh.shape["rows"]
    cols = mesh.shape["cols"]
    chips = rows // 2

    def swap(value, mask):
        return lax.ppermute(value, "rows", [(i, i ^ mask) for i in range(rows)])

    def side(value):
        pairs = [[2 * i, 2 * i + 1] for i in range(chips)]
        return lax.all_gather(
            value, "rows", axis=0, tiled=True, axis_index_groups=pairs
        )

    def trade(value, start):
        pairs = []
        for i in range(start, cols - 1, 2):
            pairs += [(i, i + 1), (i + 1, i)]
        return lax.ppermute(value, "cols", pairs)

    def on_device(iterate):
        m, n = iterate.shape
        mp = m // PIECES
        w = min(WIDTH, mp)
        q = 2 * mp // w
        z = lax.axis_index("cols")
        core = lax.axis_index("rows") % 2
        even = jnp.where(z % 2 == 0, z, cols - 1 - z)
        where = jnp.stack([even, core]).astype(jnp.int32)
        evens = range(0, cols - 1, 2)
        x0 = [
            cast(iterate, p, PIECES) for p in range(PIECES)
        ]

        groups = [(d, p) for d in range(chips) for p in range(PIECES)]
        order = [(g, i) for g in groups for i in range(q)]
        count = len(order)
        lag = SKEW * (cols - 2)
        steps = count + lag
        ready = {
            g: order.index((g, q - 1)) + lag + SKEW for g in groups
        }

        held = {}
        passing = {s: [] for s in range(steps + 1)}
        follow = {s: [] for s in range(steps + 1)}

        def hold(key, value, s):
            held[key] = value
            if 0 <= s < steps:
                passing[s].append(key)

        def then(s, action):
            if 0 <= s < steps:
                follow[s].append(action)
            else:
                late.append(action)

        late = []
        blocks = {}

        def cross(key):
            d, p = key
            end = ((d - 1) * PIECES + p + 1) * q
            hold(("x", key), swap(held.pop(("x0", key)), 2 * d), end)
            then(end, functools.partial(settle, key))

        def settle(key):
            blocks[key] = side(held.pop(("x", key)))

        for g in groups:
            d, p = g
            piece = x0[p]
            if d == 0:
                blocks[g] = side(piece)
                continue
            i = (d - 1) * PIECES + p
            begin = i * q - 1
            hold(("x0", g), piece, begin)
            if begin < 0:
                cross(g)
            else:
                then(begin, functools.partial(cross, g))

        own, sent, got_e, got_o = [], {}, {}, {}
        strip, chip, far = {}, {}, {}

        def at(values, j):
            if isinstance(values, dict):
                return (values[j], None) if j in values else None
            return values[j] if 0 <= j < len(values) else None

        def at_row(chunk):
            return jnp.full((1,), chunk, jnp.int32)

        def final(j):
            return {
                k: [at(sent, j + SKEW * k), at(got_e, j + SKEW * (cols - 2 - k))]
                for k in evens
            }

        def launch(g, s):
            d0, p = g
            strip[g] = held.pop(("s", g))
            later(("c", g), side(strip[g]), s + GAP, chip, g)
            for d in range(1, chips):
                e = d ^ d0
                if e == 0:
                    continue
                over = swap(strip[g], 2 * d)
                if s + q < steps:
                    hold(("f", d, e, p), over, s + q)
                    then(s + q, functools.partial(land, d, e, p, s + q))
                else:
                    far[d, e, p] = side(over)

        def land(d, e, p, s):
            value = side(held.pop(("f", d, e, p)))
            later(("g", d, e, p), value, s + GAP, far, (d, e, p))

        def later(key, value, s, table, place):
            if s >= steps:
                table[place] = value
                return
            hold(key, value, s)
            then(s, lambda: table.__setitem__(place, held.pop(key)))

        def target(j):
            (d, p), i = order[j]
            near = q // 2
            if d:
                column = lambda where: i
            elif i < near:
                column = lambda where: where[1] * near + i
            else:
                column = lambda where: (1 - where[1]) * near + i - near
            return held.get(("s", (d, p))), 2 * mp, column

        def turned(tile):
            per = mp // tile
            return lambda j: ((j // per) % 2 * PIECES + j // (2 * per)) * per + j % per

        def others(e, p):
            tile, stripe = ((TILE, 1024), (2 * TILE, 512))[p % 2]
            pairs = [
                (strip[d, r], c, mp, far[d, e, p], c * PIECES + r)
                for d in range(1, chips)
                for r in range(PIECES)
                for c in range(2)
            ]
            pairs += [
                (strip[0, r], c, mp, chip[e, p], c * PIECES + r)
                for r in range(PIECES)
                for c in range(2)
            ]
            return dots(
                pairs,
                2 * mp,
                min(tile, mp),
                m,
                coef_c,
                [(coef_b, [strip[e, p]])],
                jnp.bfloat16,
                stripe=stripe,
            )

        for p in range(1, PIECES):
            begin = order.index(((0, p), 0))
            hold(("r", p, 0), at_row(0), begin - 2)
            hold(("r", p, 1), at_row((1 - core) * (q // 2)), begin + q // 2 - 2)

        token = jnp.zeros((8, 128), jnp.float32)
        for s in range(steps):
            if s < count:
                g, i = order[s]
                d, p = g
                near = q // 2
                made = None
                if d == 0 and i == 0:
                    row = held.pop(("r", p, 0)) if p else at_row(0)
                    made = gram(x0, x0[p], row, near, w)
                elif d == 0 and i == near:
                    row = held.pop(("r", p, 1)) if p else at_row((1 - core) * near)
                    made = gram(x0, blocks[g], row, near, w)
                elif d > 0 and i == 0:
                    made = gram(x0, blocks[g], at_row(0), q, w)
                if made is not None:
                    own += [(made, c) for c in range(made.shape[0])]
            last_e, last_o = at(got_e, s - SKEW), at(got_o, s - SKEW)
            sums = [
                {
                    k: [at(own, s - SKEW * k)] + ([last_o] if k else [])
                    for k in evens
                }
            ]
            if SKEW <= s < count + SKEW * (cols - 3):
                sums.append(
                    {
                        k: [at(own, s - SKEW * (cols - 1 - k)), last_e] if k else []
                        for k in evens
                    }
                )
            sends = len(sums)
            j = s - lag - SKEW
            if j >= 0:
                sums.append(final(j))
            keys = passing[s]
            out = mix(
                where,
                sums,
                [held[k] for k in keys] + [token],
                PARTS,
                target(j) if j >= 0 else None,
            )
            if j >= 0:
                held["s", order[j][0]] = out[sends]
            token = out[-1]
            sent[s] = out[0]
            got_e[s] = trade(out[0], 0)
            if sends > 1:
                got_o[s] = trade(out[1], 1)
            for k, v in zip(keys, out[len(sums) : -1]):
                held[k] = v
            for g in groups:
                if ready[g] == s:
                    wait = 1 if g[0] == 0 and g[1] and s + 1 < steps else 0
                    if wait:
                        passing[s + 1].append(("s", g))
                        follow[s + 1].append(functools.partial(launch, g, s + 1))
                    else:
                        launch(g, s)
            for action in follow[s]:
                action()
        for action in late:
            action()

        for g in groups:
            if g in strip:
                continue
            for i in range(q):
                j = order.index((g, i))
                if j + lag + SKEW >= steps:
                    out = mix(where, [final(j)], [], PARTS, target(j))
                    held["s", g] = out[0]
            launch(g, steps)

        poly = {(e, p): others(e, p) for p in range(PIECES) for e in range(1, chips)}
        tile = min(2 * TILE, mp)
        first = dots(
            [(strip[g], 0, 2 * mp, chip[g], turned(tile)) for g in groups],
            2 * m,
            tile,
            m,
            coef_c,
            [(coef_b, [strip[0, p] for p in range(PIECES)])],
            jnp.bfloat16,
            stripe=1024,
        )
        factor = 0.2 * math.sqrt(max(HEIGHT, BREADTH))
        return dots(
            [(first, p, 2 * mp, blocks[0, p], 0) for p in range(PIECES)]
            + [(poly[g], 0, 2 * mp, blocks[g], 0) for g in groups if g[0]],
            n,
            TILE,
            m,
            1.0,
            [(coef_a, [iterate])],
            jnp.float32,
            factor,
            stripe=1024,
        )

    return jax.shard_map(
        on_device,
        mesh=mesh,
        in_specs=(P(("groups", "rows"), "cols"),),
        out_specs=P(("groups", "rows"), "cols"),
        check_vma=False,
    )
```

```python
import functools
import math

import jax
import jax.numpy as jnp
from jax import lax
from jax.experimental import pallas as pl
from jax.experimental.pallas import tpu as pltpu
from jax.sharding import PartitionSpec as P

HEIGHT = 4096
BREADTH = 8192

coef_a = 3.4445
coef_b = -4.775
coef_c = 2.0315

PIECES = 2
WIDTH = 256
SKEW = 2
TILE = 256
GAP = 4
VMEM = 60 * 1024 * 1024
SMALL = VMEM
PARTS = 2

NN = (((1,), (0,)), ((), ()))
NT = (((1,), (1,)), ((), ()))


def dots_body(flips, scales, spans, out_scale, height, *refs):
    count = len(flips)
    tile_at = pl.program_id(0)
    pairs, adds, out = refs[: 2 * count], refs[2 * count : -1], refs[-1]
    for start in range(0, out.shape[0], height):
        here = pl.ds(start, height)
        total = None
        for k in range(count):
            term = lax.dot_general(
                pairs[2 * k][here, :],
                pairs[2 * k + 1][...],
                NT if flips[k] else NN,
                preferred_element_type=jnp.float32,
            )
            total = term if total is None else total + term
        if scales[0] != 1.0:
            total = scales[0] * total
        left = list(adds)
        for scale, (number, span) in zip(scales[1:], spans):
            value = left.pop(0)[here, :]
            for k in range(1, number):
                value = jnp.where(tile_at < k * span, value, left.pop(0)[here, :])
            value = value.astype(jnp.float32)
            total = total + (value if scale == 1.0 else scale * value)
        if out_scale != 1.0:
            total = out_scale * total
        out[here, :] = total.astype(out.dtype)


def dots(pairs, width, tile, high, dot_scale, adds, out_dtype, out_scale=1.0, stripe=512):
    m = pairs[0][0].shape[0]
    high, once = min(high, m), {}
    if high == m:
        once["pipeline_mode"] = pl.Buffered(1)
    operands, specs, flips = [], [], []
    flops = 0
    for left, column, depth, right, where in pairs:
        operands += [left, right]
        specs.append(
            pl.BlockSpec(
                (high, depth), functools.partial(lambda c, j, i: (i, c), column), **once
            )
        )
        flip = callable(where)
        if flip:
            specs.append(
                pl.BlockSpec(
                    (tile, depth), functools.partial(lambda f, j, i: (f(j), 0), where)
                )
            )
        else:
            specs.append(
                pl.BlockSpec(
                    (depth, tile), functools.partial(lambda b, j, i: (b, j), where)
                )
            )
        flips.append(flip)
        flops += 2 * m * depth * width
    spans = []
    for _, joined in adds:
        span = joined[0].shape[1] // tile
        spans.append((len(joined), span))
        for k, add in enumerate(joined):
            operands.append(add)
            specs.append(
                pl.BlockSpec(
                    (high, tile),
                    functools.partial(
                        lambda f, t, j, i: (i, jnp.clip(j - f, 0, t - 1)), k * span, span
                    ),
                )
            )
    return pl.pallas_call(
        functools.partial(
            dots_body,
            tuple(flips),
            (dot_scale,) + tuple(s for s, _ in adds),
            tuple(spans),
            out_scale,
            min(stripe, high),
        ),
        out_shape=jax.ShapeDtypeStruct((m, width), out_dtype),
        grid=(width // tile, m // high),
        in_specs=specs,
        out_specs=pl.BlockSpec((high, tile), lambda j, i: (i, j)),
        compiler_params=pltpu.CompilerParams(vmem_limit_bytes=VMEM),
        cost_estimate=pl.CostEstimate(
            flops=flops, bytes_accessed=0, transcendentals=0
        ),
    )(*operands)


def gram_body(where, *refs):
    *lefts, right, out = refs
    high = lefts[0].shape[0]
    for k, left in enumerate(lefts):
        out[0, k * high : (k + 1) * high, :] = lax.dot_general(
            left[...], right[...], NT, preferred_element_type=jnp.float32
        ).astype(out.dtype)


def gram(lefts, right, where, count, width):
    high, n = lefts[0].shape
    m = high * len(lefts)
    return pl.pallas_call(
        gram_body,
        out_shape=jax.ShapeDtypeStruct((count, m, width), jnp.bfloat16),
        grid_spec=pltpu.PrefetchScalarGridSpec(
            num_scalar_prefetch=1,
            grid=(count,),
            in_specs=[
                pl.BlockSpec(
                    (high, n), lambda j, where: (0, 0), pipeline_mode=pl.Buffered(1)
                )
            ]
            * len(lefts)
            + [pl.BlockSpec((width, n), lambda j, where: (where[0] + j, 0))],
            out_specs=pl.BlockSpec((1, m, width), lambda j, where: (j, 0, 0)),
        ),
        compiler_params=pltpu.CompilerParams(vmem_limit_bytes=VMEM),
        cost_estimate=pl.CostEstimate(
            flops=2 * m * n * width * count, bytes_accessed=0, transcendentals=0
        ),
    )(where, *lefts, right)


def mix_body(plan, count, idle, where, *refs):
    ins, outs = refs[:count], refs[count + idle :]
    for k, sums in plan:

        @pl.when(where[0] == k)
        def _():
            for out, slots in zip(outs, sums):
                total = None
                for slot in slots:
                    value = ins[slot][...].reshape(out.shape)
                    total = value if total is None else total + value
                if total is not None:
                    out[...] = total


def mix(where, sums, held, parts, strip=None):
    sources, uses = [], []
    kinds = sorted(sums[0])
    plan = []
    for k in kinds:
        row = []
        for terms in sums:
            slots = []
            for source in terms[k]:
                if source is None:
                    continue
                for slot, (array, chunk) in enumerate(sources):
                    if array is source[0] and chunk == source[1]:
                        break
                else:
                    slot = len(sources)
                    sources.append(source)
                    uses.append(set())
                uses[slot].add(k)
                slots.append(slot)
            row.append(tuple(slots))
        plan.append((k, tuple(row)))
    m, w = sources[0][0].shape[-2:]
    high = m // parts
    specs = []
    for (array, chunk), used in zip(sources, uses):

        def at(j, where, chunk=chunk, used=tuple(sorted(used))):
            row = j
            if len(used) < len(kinds):
                live = where[0] == used[0]
                for k in used[1:]:
                    live = live | (where[0] == k)
                row = jnp.where(live, j, 0)
            return (row, 0) if chunk is None else (chunk, row, 0)

        specs.append(pl.BlockSpec((high, w) if chunk is None else (1, high, w), at))
    anywhere = pl.BlockSpec(memory_space=pl.ANY)
    shapes = [jax.ShapeDtypeStruct((m, w), jnp.bfloat16)] * len(sums)
    outs = [pl.BlockSpec((high, w), lambda j, where: (j, 0))] * len(sums)
    passed = list(held)
    alias = [len(sums) + k for k in range(len(held))]
    if strip is not None:
        before, width, column = strip
        shapes[-1] = jax.ShapeDtypeStruct((m, width), jnp.bfloat16)
        outs[-1] = pl.BlockSpec((high, w), lambda j, where: (j, column(where)))
        if before is not None:
            passed.append(before)
            alias.append(len(sums) - 1)
    idle, count = len(passed), len(sources)
    return list(
        pl.pallas_call(
            functools.partial(mix_body, tuple(plan), count, idle),
            out_shape=shapes
            + [jax.ShapeDtypeStruct(v.shape, v.dtype) for v in held],
            grid_spec=pltpu.PrefetchScalarGridSpec(
                num_scalar_prefetch=1,
                grid=(parts,),
                in_specs=specs + [anywhere] * idle,
                out_specs=outs + [anywhere] * len(held),
            ),
            input_output_aliases={1 + count + k: a for k, a in enumerate(alias)},
            compiler_params=pltpu.CompilerParams(vmem_limit_bytes=SMALL),
            cost_estimate=pl.CostEstimate(
                flops=4 * 10**10, bytes_accessed=0, transcendentals=0
            ),
        )(where, *[a for a, _ in sources], *passed)
    )


def solution(mesh):
    rows = mesh.shape["rows"]
    cols = mesh.shape["cols"]
    chips = rows // 2

    def swap(value, mask):
        return lax.ppermute(value, "rows", [(i, i ^ mask) for i in range(rows)])

    def side(value):
        pairs = [[2 * i, 2 * i + 1] for i in range(chips)]
        return lax.all_gather(
            value, "rows", axis=0, tiled=True, axis_index_groups=pairs
        )

    def trade(value, start):
        pairs = []
        for i in range(start, cols - 1, 2):
            pairs += [(i, i + 1), (i + 1, i)]
        return lax.ppermute(value, "cols", pairs)

    def on_device(iterate):
        m, n = iterate.shape
        mp = m // PIECES
        w = min(WIDTH, mp)
        q = 2 * mp // w
        z = lax.axis_index("cols")
        core = lax.axis_index("rows") % 2
        even = jnp.where(z % 2 == 0, z, cols - 1 - z)
        where = jnp.stack([even, core]).astype(jnp.int32)
        evens = range(0, cols - 1, 2)
        x0 = [
            iterate[p * mp : (p + 1) * mp].astype(jnp.bfloat16) for p in range(PIECES)
        ]

        groups = [(d, p) for d in range(chips) for p in range(PIECES)]
        order = [(g, i) for g in groups for i in range(q)]
        count = len(order)
        lag = SKEW * (cols - 2)
        steps = count + lag
        ready = {
            g: order.index((g, q - 1)) + lag + SKEW for g in groups
        }

        held = {}
        passing = {s: [] for s in range(steps + 1)}
        follow = {s: [] for s in range(steps + 1)}

        def hold(key, value, s):
            held[key] = value
            if 0 <= s < steps:
                passing[s].append(key)

        def then(s, action):
            if 0 <= s < steps:
                follow[s].append(action)
            else:
                late.append(action)

        late = []
        blocks = {}

        def cross(key):
            d, p = key
            end = ((d - 1) * PIECES + p + 1) * q
            hold(("x", key), swap(held.pop(("x0", key)), 2 * d), end)
            then(end, functools.partial(settle, key))

        def settle(key):
            blocks[key] = side(held.pop(("x", key)))

        for g in groups:
            d, p = g
            piece = x0[p]
            if d == 0:
                blocks[g] = side(piece)
                continue
            i = (d - 1) * PIECES + p
            begin = i * q - 1
            hold(("x0", g), piece, begin)
            if begin < 0:
                cross(g)
            else:
                then(begin, functools.partial(cross, g))

        own, sent, got_e, got_o = [], {}, {}, {}
        strip, chip, far = {}, {}, {}

        def at(values, j):
            if isinstance(values, dict):
                return (values[j], None) if j in values else None
            return values[j] if 0 <= j < len(values) else None

        def at_row(chunk):
            return jnp.full((1,), chunk, jnp.int32)

        def final(j):
            return {
                k: [at(sent, j + SKEW * k), at(got_e, j + SKEW * (cols - 2 - k))]
                for k in evens
            }

        def launch(g, s):
            d0, p = g
            strip[g] = held.pop(("s", g))
            hidden = g == (0, PIECES - 1) and s + GAP < steps
            later(("c", g), side(strip[g]), steps - 1 if hidden else s + GAP, chip, g)
            for d in range(1, chips):
                e = d ^ d0
                if e == 0:
                    continue
                over = swap(strip[g], 2 * d)
                if s + q < steps:
                    hold(("f", d, e, p), over, s + q)
                    then(s + q, functools.partial(land, d, e, p, s + q))
                else:
                    far[d, e, p] = side(over)

        def land(d, e, p, s):
            value = side(held.pop(("f", d, e, p)))
            later(("g", d, e, p), value, s + GAP, far, (d, e, p))

        def later(key, value, s, table, place):
            if s >= steps:
                table[place] = value
                return
            hold(key, value, s)
            then(s, lambda: table.__setitem__(place, held.pop(key)))

        def target(j):
            (d, p), i = order[j]
            near = q // 2
            if d:
                column = lambda where: i
            elif i < near:
                column = lambda where: where[1] * near + i
            else:
                column = lambda where: (1 - where[1]) * near + i - near
            return held.get(("s", (d, p))), 2 * mp, column

        def turned(tile):
            per = mp // tile
            return lambda j: ((j // per) % 2 * PIECES + j // (2 * per)) * per + j % per

        def others(e, p):
            tile, stripe = ((TILE, 1024), (2 * TILE, 512))[p % 2]
            pairs = [
                (strip[d, r], c, mp, far[d, e, p], c * PIECES + r)
                for d in range(1, chips)
                for r in range(PIECES)
                for c in range(2)
            ]
            pairs += [
                (strip[0, r], c, mp, chip[e, p], c * PIECES + r)
                for r in range(PIECES)
                for c in range(2)
            ]
            return dots(
                pairs,
                2 * mp,
                min(tile, mp),
                m,
                coef_c,
                [(coef_b, [strip[e, p]])],
                jnp.bfloat16,
                stripe=stripe,
            )

        for p in range(1, PIECES):
            begin = order.index(((0, p), 0))
            hold(("r", p, 0), at_row(0), begin - 2)
            hold(("r", p, 1), at_row((1 - core) * (q // 2)), begin + q // 2 - 2)

        token = jnp.zeros((8, 128), jnp.float32)
        for s in range(steps):
            if s < count:
                g, i = order[s]
                d, p = g
                near = q // 2
                made = None
                if d == 0 and i == 0:
                    row = held.pop(("r", p, 0)) if p else at_row(0)
                    made = gram(x0, x0[p], row, near, w)
                elif d == 0 and i == near:
                    row = held.pop(("r", p, 1)) if p else at_row((1 - core) * near)
                    made = gram(x0, blocks[g], row, near, w)
                elif d > 0 and i == 0:
                    made = gram(x0, blocks[g], at_row(0), q, w)
                if made is not None:
                    own += [(made, c) for c in range(made.shape[0])]
            last_e, last_o = at(got_e, s - SKEW), at(got_o, s - SKEW)
            sums = [
                {
                    k: [at(own, s - SKEW * k)] + ([last_o] if k else [])
                    for k in evens
                }
            ]
            if SKEW <= s < count + SKEW * (cols - 3):
                sums.append(
                    {
                        k: [at(own, s - SKEW * (cols - 1 - k)), last_e] if k else []
                        for k in evens
                    }
                )
            sends = len(sums)
            j = s - lag - SKEW
            if j >= 0:
                sums.append(final(j))
            keys = passing[s]
            out = mix(
                where,
                sums,
                [held[k] for k in keys] + [token],
                PARTS,
                target(j) if j >= 0 else None,
            )
            if j >= 0:
                held["s", order[j][0]] = out[sends]
            token = out[-1]
            sent[s] = out[0]
            got_e[s] = trade(out[0], 0)
            if sends > 1:
                got_o[s] = trade(out[1], 1)
            for k, v in zip(keys, out[len(sums) : -1]):
                held[k] = v
            for g in groups:
                if ready[g] == s:
                    wait = 1 if g[0] == 0 and g[1] and s + 1 < steps else 0
                    if wait:
                        passing[s + 1].append(("s", g))
                        follow[s + 1].append(functools.partial(launch, g, s + 1))
                    else:
                        launch(g, s)
            for action in follow[s]:
                action()
        for action in late:
            action()

        tile = min(2 * TILE, mp)

        def first(part, adds, dtype):
            return dots(
                [(strip[g], 0, 2 * mp, chip[g], turned(tile)) for g in part],
                2 * m,
                tile,
                m,
                coef_c,
                adds,
                dtype,
                stripe=1024,
            )

        near = groups[:PIECES]
        early = None
        if all(g in strip for g in near):
            early = first(
                near, [(coef_b, [strip[0, p] for p in range(PIECES)])], jnp.float32
            )
        for g in groups:
            if g in strip:
                continue
            for i in range(q):
                j = order.index((g, i))
                if j + lag + SKEW >= steps:
                    pass_on = [] if early is None else [early]
                    out = mix(where, [final(j)], pass_on, PARTS, target(j))
                    held["s", g] = out[0]
                    early = out[1] if pass_on else None
            launch(g, steps)

        poly = {(e, p): others(e, p) for p in range(PIECES) for e in range(1, chips)}
        if early is None:
            own_poly = first(
                groups, [(coef_b, [strip[0, p] for p in range(PIECES)])], jnp.bfloat16
            )
        else:
            own_poly = first(groups[PIECES:], [(1.0, [early])], jnp.bfloat16)
        factor = 0.2 * math.sqrt(max(HEIGHT, BREADTH))
        return dots(
            [(own_poly, p, 2 * mp, blocks[0, p], 0) for p in range(PIECES)]
            + [(poly[g], 0, 2 * mp, blocks[g], 0) for g in groups if g[0]],
            n,
            TILE,
            m,
            1.0,
            [(coef_a, [iterate])],
            jnp.float32,
            factor,
            stripe=1024,
        )

    return jax.shard_map(
        on_device,
        mesh=mesh,
        in_specs=(P(("groups", "rows"), "cols"),),
        out_specs=P(("groups", "rows"), "cols"),
        check_vma=False,
    )
```

```python
import functools
import math

import jax
import jax.numpy as jnp
from jax import lax
from jax.experimental import pallas as pl
from jax.experimental.pallas import tpu as pltpu
from jax.sharding import PartitionSpec as P

HEIGHT = 4096
BREADTH = 8192

coef_a = 3.4445
coef_b = -4.775
coef_c = 2.0315

PIECES = 2
WIDTH = 256
SKEW = 2
TILE = 256
GAP = 4
VMEM = 60 * 1024 * 1024
SMALL = VMEM
PARTS = 2

NN = (((1,), (0,)), ((), ()))
NT = (((1,), (1,)), ((), ()))


def dots_body(flips, scales, spans, out_scale, height, *refs):
    count = len(flips)
    tile_at = pl.program_id(0)
    pairs, adds, out = refs[: 2 * count], refs[2 * count : -1], refs[-1]
    for start in range(0, out.shape[0], height):
        here = pl.ds(start, height)
        total = None
        for k in range(count):
            term = lax.dot_general(
                pairs[2 * k][here, :],
                pairs[2 * k + 1][...],
                NT if flips[k] else NN,
                preferred_element_type=jnp.float32,
            )
            total = term if total is None else total + term
        if scales[0] != 1.0:
            total = scales[0] * total
        left = list(adds)
        for scale, (number, span) in zip(scales[1:], spans):
            value = left.pop(0)[here, :]
            for k in range(1, number):
                value = jnp.where(tile_at < k * span, value, left.pop(0)[here, :])
            value = value.astype(jnp.float32)
            total = total + (value if scale == 1.0 else scale * value)
        if out_scale != 1.0:
            total = out_scale * total
        out[here, :] = total.astype(out.dtype)


def dots(pairs, width, tile, high, dot_scale, adds, out_dtype, out_scale=1.0, stripe=512):
    m = pairs[0][0].shape[0]
    high, once = min(high, m), {}
    if high == m:
        once["pipeline_mode"] = pl.Buffered(1)
    operands, specs, flips = [], [], []
    flops = 0
    for left, column, depth, right, where in pairs:
        operands += [left, right]
        specs.append(
            pl.BlockSpec(
                (high, depth), functools.partial(lambda c, j, i: (i, c), column), **once
            )
        )
        flip = callable(where)
        if flip:
            specs.append(
                pl.BlockSpec(
                    (tile, depth), functools.partial(lambda f, j, i: (f(j), 0), where)
                )
            )
        else:
            specs.append(
                pl.BlockSpec(
                    (depth, tile), functools.partial(lambda b, j, i: (b, j), where)
                )
            )
        flips.append(flip)
        flops += 2 * m * depth * width
    spans = []
    for _, joined in adds:
        span = joined[0].shape[1] // tile
        spans.append((len(joined), span))
        for k, add in enumerate(joined):
            operands.append(add)
            specs.append(
                pl.BlockSpec(
                    (high, tile),
                    functools.partial(
                        lambda f, t, j, i: (i, jnp.clip(j - f, 0, t - 1)), k * span, span
                    ),
                )
            )
    return pl.pallas_call(
        functools.partial(
            dots_body,
            tuple(flips),
            (dot_scale,) + tuple(s for s, _ in adds),
            tuple(spans),
            out_scale,
            min(stripe, high),
        ),
        out_shape=jax.ShapeDtypeStruct((m, width), out_dtype),
        grid=(width // tile, m // high),
        in_specs=specs,
        out_specs=pl.BlockSpec((high, tile), lambda j, i: (i, j)),
        compiler_params=pltpu.CompilerParams(vmem_limit_bytes=VMEM),
        cost_estimate=pl.CostEstimate(
            flops=flops, bytes_accessed=0, transcendentals=0
        ),
    )(*operands)


def gram_body(where, *refs):
    *lefts, right, out = refs
    high = lefts[0].shape[0]
    for k, left in enumerate(lefts):
        out[0, k * high : (k + 1) * high, :] = lax.dot_general(
            left[...], right[...], NT, preferred_element_type=jnp.float32
        ).astype(out.dtype)


def gram(lefts, right, where, count, width):
    high, n = lefts[0].shape
    m = high * len(lefts)
    return pl.pallas_call(
        gram_body,
        out_shape=jax.ShapeDtypeStruct((count, m, width), jnp.bfloat16),
        grid_spec=pltpu.PrefetchScalarGridSpec(
            num_scalar_prefetch=1,
            grid=(count,),
            in_specs=[
                pl.BlockSpec(
                    (high, n), lambda j, where: (0, 0), pipeline_mode=pl.Buffered(1)
                )
            ]
            * len(lefts)
            + [pl.BlockSpec((width, n), lambda j, where: (where[0] + j, 0))],
            out_specs=pl.BlockSpec((1, m, width), lambda j, where: (j, 0, 0)),
        ),
        compiler_params=pltpu.CompilerParams(vmem_limit_bytes=VMEM),
        cost_estimate=pl.CostEstimate(
            flops=2 * m * n * width * count, bytes_accessed=0, transcendentals=0
        ),
    )(where, *lefts, right)


def mix_body(plan, count, idle, where, *refs):
    ins, outs = refs[:count], refs[count + idle :]
    for k, sums in plan:

        @pl.when(where[0] == k)
        def _():
            for out, slots in zip(outs, sums):
                total = None
                for slot in slots:
                    value = ins[slot][...].reshape(out.shape)
                    total = value if total is None else total + value
                if total is not None:
                    out[...] = total


def mix(where, sums, held, parts, strip=None):
    sources, uses = [], []
    kinds = sorted(sums[0])
    plan = []
    for k in kinds:
        row = []
        for terms in sums:
            slots = []
            for source in terms[k]:
                if source is None:
                    continue
                for slot, (array, chunk) in enumerate(sources):
                    if array is source[0] and chunk == source[1]:
                        break
                else:
                    slot = len(sources)
                    sources.append(source)
                    uses.append(set())
                uses[slot].add(k)
                slots.append(slot)
            row.append(tuple(slots))
        plan.append((k, tuple(row)))
    m, w = sources[0][0].shape[-2:]
    high = m // parts
    specs = []
    for (array, chunk), used in zip(sources, uses):

        def at(j, where, chunk=chunk, used=tuple(sorted(used))):
            row = j
            if len(used) < len(kinds):
                live = where[0] == used[0]
                for k in used[1:]:
                    live = live | (where[0] == k)
                row = jnp.where(live, j, 0)
            return (row, 0) if chunk is None else (chunk, row, 0)

        specs.append(pl.BlockSpec((high, w) if chunk is None else (1, high, w), at))
    anywhere = pl.BlockSpec(memory_space=pl.ANY)
    shapes = [jax.ShapeDtypeStruct((m, w), jnp.bfloat16)] * len(sums)
    outs = [pl.BlockSpec((high, w), lambda j, where: (j, 0))] * len(sums)
    passed = list(held)
    alias = [len(sums) + k for k in range(len(held))]
    if strip is not None:
        before, width, column = strip
        shapes[-1] = jax.ShapeDtypeStruct((m, width), jnp.bfloat16)
        outs[-1] = pl.BlockSpec((high, w), lambda j, where: (j, column(where)))
        if before is not None:
            passed.append(before)
            alias.append(len(sums) - 1)
    idle, count = len(passed), len(sources)
    return list(
        pl.pallas_call(
            functools.partial(mix_body, tuple(plan), count, idle),
            out_shape=shapes
            + [jax.ShapeDtypeStruct(v.shape, v.dtype) for v in held],
            grid_spec=pltpu.PrefetchScalarGridSpec(
                num_scalar_prefetch=1,
                grid=(parts,),
                in_specs=specs + [anywhere] * idle,
                out_specs=outs + [anywhere] * len(held),
            ),
            input_output_aliases={1 + count + k: a for k, a in enumerate(alias)},
            compiler_params=pltpu.CompilerParams(vmem_limit_bytes=SMALL),
            cost_estimate=pl.CostEstimate(
                flops=4 * 10**10, bytes_accessed=0, transcendentals=0
            ),
        )(where, *[a for a, _ in sources], *passed)
    )


def solution(mesh):
    rows = mesh.shape["rows"]
    cols = mesh.shape["cols"]
    chips = rows // 2

    def swap(value, mask):
        return lax.ppermute(value, "rows", [(i, i ^ mask) for i in range(rows)])

    def side(value):
        pairs = [[2 * i, 2 * i + 1] for i in range(chips)]
        return lax.all_gather(
            value, "rows", axis=0, tiled=True, axis_index_groups=pairs
        )

    def trade(value, start):
        pairs = []
        for i in range(start, cols - 1, 2):
            pairs += [(i, i + 1), (i + 1, i)]
        return lax.ppermute(value, "cols", pairs)

    def on_device(iterate):
        m, n = iterate.shape
        mp = m // PIECES
        w = min(WIDTH, mp)
        q = 2 * mp // w
        z = lax.axis_index("cols")
        core = lax.axis_index("rows") % 2
        even = jnp.where(z % 2 == 0, z, cols - 1 - z)
        where = jnp.stack([even, core]).astype(jnp.int32)
        evens = range(0, cols - 1, 2)
        x0 = [
            iterate[p * mp : (p + 1) * mp].astype(jnp.bfloat16) for p in range(PIECES)
        ]

        groups = [(d, p) for d in range(chips) for p in range(PIECES)]
        order = [(g, i) for g in groups for i in range(q)]
        count = len(order)
        lag = SKEW * (cols - 2)
        steps = count + lag
        ready = {
            g: order.index((g, q - 1)) + lag + SKEW for g in groups
        }

        held = {}
        passing = {s: [] for s in range(steps + 1)}
        follow = {s: [] for s in range(steps + 1)}

        def hold(key, value, s):
            held[key] = value
            if 0 <= s < steps:
                passing[s].append(key)

        def then(s, action):
            if 0 <= s < steps:
                follow[s].append(action)
            else:
                late.append(action)

        late = []
        blocks = {}

        def cross(key):
            d, p = key
            end = ((d - 1) * PIECES + p + 1) * q
            hold(("x", key), swap(held.pop(("x0", key)), 2 * d), end)
            then(end, functools.partial(settle, key))

        def settle(key):
            blocks[key] = side(held.pop(("x", key)))

        for g in groups:
            d, p = g
            piece = x0[p]
            if d == 0:
                blocks[g] = side(piece)
                continue
            i = (d - 1) * PIECES + p
            begin = i * q - 1
            hold(("x0", g), piece, begin)
            if begin < 0:
                cross(g)
            else:
                then(begin, functools.partial(cross, g))

        own, sent, got_e, got_o = [], {}, {}, {}
        strip, chip, far = {}, {}, {}

        def at(values, j):
            if isinstance(values, dict):
                return (values[j], None) if j in values else None
            return values[j] if 0 <= j < len(values) else None

        def at_row(chunk):
            return jnp.full((1,), chunk, jnp.int32)

        def final(j):
            return {
                k: [at(sent, j + SKEW * k), at(got_e, j + SKEW * (cols - 2 - k))]
                for k in evens
            }

        def launch(g, s):
            d0, p = g
            strip[g] = held.pop(("s", g))
            later(("c", g), side(strip[g]), s + GAP, chip, g)
            for d in range(1, chips):
                e = d ^ d0
                if e == 0:
                    continue
                over = swap(strip[g], 2 * d)
                if s + q + p < steps:
                    hold(("f", d, e, p), over, s + q + p)
                    then(s + q + p, functools.partial(land, d, e, p, s + q + p))
                else:
                    far[d, e, p] = side(over)

        def land(d, e, p, s):
            value = side(held.pop(("f", d, e, p)))
            later(("g", d, e, p), value, s + GAP, far, (d, e, p))

        def later(key, value, s, table, place):
            if s >= steps:
                table[place] = value
                return
            hold(key, value, s)
            then(s, lambda: table.__setitem__(place, held.pop(key)))

        def target(j):
            (d, p), i = order[j]
            near = q // 2
            if d:
                column = lambda where: i
            elif i < near:
                column = lambda where: where[1] * near + i
            else:
                column = lambda where: (1 - where[1]) * near + i - near
            return held.get(("s", (d, p))), 2 * mp, column

        def turned(tile):
            per = mp // tile
            return lambda j: ((j // per) % 2 * PIECES + j // (2 * per)) * per + j % per

        def others(e, p):
            tile, stripe = TILE, 512
            pairs = [
                (strip[d, r], c, mp, far[d, e, p], c * PIECES + r)
                for d in range(1, chips)
                for r in range(PIECES)
                for c in range(2)
            ]
            pairs += [
                (strip[0, r], c, mp, chip[e, p], c * PIECES + r)
                for r in range(PIECES)
                for c in range(2)
            ]
            return dots(
                pairs,
                2 * mp,
                min(tile, mp),
                m,
                coef_c,
                [(coef_b, [strip[e, p]])],
                jnp.bfloat16,
                stripe=stripe,
            )

        for p in range(1, PIECES):
            begin = order.index(((0, p), 0))
            hold(("r", p, 0), at_row(0), begin - 2)
            hold(("r", p, 1), at_row((1 - core) * (q // 2)), begin + q // 2 - 2)

        token = jnp.zeros((8, 128), jnp.float32)
        for s in range(steps):
            if s < count:
                g, i = order[s]
                d, p = g
                near = q // 2
                made = None
                if d == 0 and i == 0:
                    row = held.pop(("r", p, 0)) if p else at_row(0)
                    made = gram(x0, x0[p], row, near, w)
                elif d == 0 and i == near:
                    row = held.pop(("r", p, 1)) if p else at_row((1 - core) * near)
                    made = gram(x0, blocks[g], row, near, w)
                elif d > 0 and i == 0:
                    made = gram(x0, blocks[g], at_row(0), q, w)
                if made is not None:
                    own += [(made, c) for c in range(made.shape[0])]
            last_e, last_o = at(got_e, s - SKEW), at(got_o, s - SKEW)
            sums = [
                {
                    k: [at(own, s - SKEW * k)] + ([last_o] if k else [])
                    for k in evens
                }
            ]
            if SKEW <= s < count + SKEW * (cols - 3):
                sums.append(
                    {
                        k: [at(own, s - SKEW * (cols - 1 - k)), last_e] if k else []
                        for k in evens
                    }
                )
            sends = len(sums)
            j = s - lag - SKEW
            if j >= 0:
                sums.append(final(j))
            keys = list(passing[s])
            out = mix(
                where,
                sums,
                [held[k] for k in keys] + [token],
                PARTS,
                target(j) if j >= 0 else None,
            )
            if j >= 0:
                held["s", order[j][0]] = out[sends]
            token = out[-1]
            sent[s] = out[0]
            got_e[s] = trade(out[0], 0)
            if sends > 1:
                got_o[s] = trade(out[1], 1)
            for k, v in zip(keys, out[len(sums) : -1]):
                held[k] = v
            for g in groups:
                if ready[g] == s:
                    wait = 1 if g[0] == 0 and g[1] and s + 1 < steps else 0
                    if wait:
                        passing[s + 1].append(("s", g))
                        follow[s + 1].append(functools.partial(launch, g, s + 1))
                    else:
                        launch(g, s)
            for action in follow[s]:
                action()
        for action in late:
            action()

        tile = min(2 * TILE, mp)

        def first(part, adds, dtype):
            return dots(
                [(strip[g], 0, 2 * mp, chip[g], turned(tile)) for g in part],
                2 * m,
                tile,
                m,
                coef_c,
                adds,
                dtype,
                stripe=1024,
            )

        near = groups[:PIECES]
        early = None
        if all(g in strip for g in near):
            early = first(
                near, [(coef_b, [strip[0, p] for p in range(PIECES)])], jnp.float32
            )
        for g in groups:
            if g in strip:
                continue
            for i in range(q):
                j = order.index((g, i))
                if j + lag + SKEW >= steps:
                    pass_on = [] if early is None else [early]
                    out = mix(where, [final(j)], pass_on, PARTS, target(j))
                    held["s", g] = out[0]
                    early = out[1] if pass_on else None
            launch(g, steps)

        poly = {(e, p): others(e, p) for p in range(PIECES) for e in range(1, chips)}
        if early is None:
            own_poly = first(
                groups, [(coef_b, [strip[0, p] for p in range(PIECES)])], jnp.bfloat16
            )
        else:
            own_poly = first(groups[PIECES:], [(1.0, [early])], jnp.bfloat16)
        factor = 0.2 * math.sqrt(max(HEIGHT, BREADTH))
        return dots(
            [(own_poly, p, 2 * mp, blocks[0, p], 0) for p in range(PIECES)]
            + [(poly[g], 0, 2 * mp, blocks[g], 0) for g in groups if g[0]],
            n,
            TILE,
            m,
            1.0,
            [(coef_a, [iterate])],
            jnp.float32,
            factor,
            stripe=1024,
        )

    return jax.shard_map(
        on_device,
        mesh=mesh,
        in_specs=(P(("groups", "rows"), "cols"),),
        out_specs=P(("groups", "rows"), "cols"),
        check_vma=False,
    )
```
